128 devices in a mesh: gauss: 4 (over x), pix: 32 (over y, z, core).
Axes of the slice: x: 4, y: 4, z: 4, core: 2. Of those that a mesh axis runs over, the one named last changes fastest.
Arguments:
- params: float32 [54, 2097152], P(None, ('gauss', 'pix')), may hold values from -8 to 22, as said below
- angles_next: float32 [2048, 2], P(('gauss', 'pix')), may hold values from -3.140625 to 3.140625
- angles_cur: float32 [2048, 2], P(('gauss', 'pix')), may hold values from -3.140625 to 3.140625
- lists_next: int32 [2048, 256], P(('gauss', 'pix')), may hold values from 0 to 4095, as said below
- lists_cur: int32 [2048, 256], P(('gauss', 'pix')), may hold values from 0 to 4095, as said below
- counts_next: int32 [2048], P(('gauss', 'pix')), may hold values from 97 to 256, as said below
- counts_cur: int32 [2048], P(('gauss', 'pix')), may hold values from 97 to 256, as said below
- sends_next: int32 [128, 128, 32], P(('gauss', 'pix')), may hold values from 0 to 16383
- sends_cur: int32 [128, 128, 32], P(('gauss', 'pix')), may hold values from 0 to 16383
- cotangent: float32 [2048, 3, 256], P(('gauss', 'pix')), may hold values from -6 to 6
Outputs:
- image_next: float32 [2048, 3, 256], P(('gauss', 'pix'))
- grads: float32 [54, 2097152], P(None, ('gauss', 'pix'))
The draws below stay inside these ranges and needn't reach their ends.
Inputs may be any that keep to these rules, and one draw needn't show every extreme that they name: `params`: gaussian parameters: rows 2 and 4 (conic diagonal) lie in 0.01 to 0.1, row 3 below 0.8 sqrt(row 2 * row 4) in magnitude, row 5 in -8 to 5. `lists_next`: within the 16 tiles of one device, every slot of that device appears exactly once among all entries, live or padding. `lists_cur`: within the 16 tiles of one device, every slot of that device appears exactly once among all entries, live or padding. `counts_next`: live entries at the front of each tile's list; the rest is padding. `counts_cur`: live entries at the front of each tile's list; the rest is padding.
All inputs are finite; a program needn't handle non-finite values.
Results may differ from the reference program's by a relative error of at most 0.0003.
Values sent between devices are 32-bit elements; how exact they have to be, the bound alone decides.
A program may use at most 128 MiB of HBM per device.

```python
import math
import jax
import jax.numpy as jnp
from jax import lax

TILE_DEV = 16
BLOCKS = 2
GAUSS_DEV = 16384
TILE_PIX = 256
SLOTS = 32
TILES = 2048
GAUSSIANS = 2097152
DEVICES = 128


def draw_params(key, part):
    key = jax.random.fold_in(key, 7)
    keys = jax.random.split(key, 9)
    total = GAUSSIANS
    centers = jax.random.uniform(keys[0], (2, total), jnp.float32, -4.0, 20.0)
    base = 0.5 * jnp.clip(jax.random.normal(keys[1], (3, 1, total), jnp.float32), -3.0, 3.0)
    higher = 0.2 * jnp.clip(jax.random.normal(keys[2], (3, 15, total), jnp.float32), -3.0, 3.0)
    con_a = jnp.exp(jax.random.uniform(keys[3], (1, total), jnp.float32, math.log(0.01), math.log(0.1)))
    con_c = jnp.exp(jax.random.uniform(keys[4], (1, total), jnp.float32, math.log(0.01), math.log(0.1)))
    con_b = jax.random.uniform(keys[5], (1, total), jnp.float32, -0.8, 0.8) * jnp.sqrt(con_a * con_c)
    faint = jax.random.uniform(keys[6], (1, total), jnp.float32, -8.0, -3.0)
    solid = jax.random.uniform(keys[7], (1, total), jnp.float32, 0.0, 5.0)
    pick = jax.random.uniform(keys[8], (1, total), jnp.float32, 0.0, 1.0)
    logit = jnp.where(pick < 1.0 / 64.0, solid, faint)
    harmonics = jnp.concatenate([base, higher], 1).reshape(48, total)
    return jnp.concatenate([centers, con_a, con_b, con_c, logit, harmonics], 0)


def drawn_live(key):
    limit = BLOCKS * 128
    owner = jnp.arange(TILES) // TILE_DEV
    light = (jax.random.randint(jax.random.fold_in(key, 1), (DEVICES,), 0, 4) == 0)[owner]
    top = jnp.where(light, limit // 2, limit)
    raw = jax.random.randint(jax.random.fold_in(key, 2), (TILES,), 0, 1 << 20)
    live = top - raw % (top // 4)
    live = live.at[0].set(limit).at[TILES - 1].set(3 * limit // 8 + 1)
    return live.astype(jnp.int32)


def shuffled_entries(key):
    span = TILE_DEV * BLOCKS * 128
    keys = jax.random.split(key, DEVICES)
    perms = jax.vmap(lambda one: jax.random.permutation(one, span))(keys)
    ordered = jnp.transpose(perms.reshape(DEVICES, BLOCKS * 128, TILE_DEV), (0, 2, 1))
    return ordered.reshape(TILES, BLOCKS * 128).astype(jnp.int32)


def draw_counts_next(key, part):
    key = jax.random.fold_in(key, 5)
    return drawn_live(key)


def draw_counts_cur(key, part):
    key = jax.random.fold_in(key, 9)
    return drawn_live(key)


def draw_lists_next(key, part):
    key = jax.random.fold_in(key, 11)
    return shuffled_entries(key)


def draw_lists_cur(key, part):
    key = jax.random.fold_in(key, 13)
    return shuffled_entries(key)


def touch_ends(array, own_key, smallest, top_value):
    longest = array.shape.index(max(array.shape))
    spots = []
    for shift in (0, 1):
        where = [jax.random.randint(jax.random.fold_in(own_key, axis), (), 0, length) for axis, length in enumerate(array.shape)]
        where[longest] = (where[longest] + shift) % array.shape[longest]
        spots.append(tuple(where))
    return array.at[spots[0]].set(smallest).at[spots[1]].set(top_value)


def block_scale(stream_key, extent, shards, smallest, top_value):
    factor_of = 1.0
    for position, shards_of in shards:
        heights = jax.random.uniform(jax.random.fold_in(jax.random.fold_in(stream_key, 6), position), (shards_of,), jnp.float32, smallest / len(shards), top_value / len(shards))
        factor_of = factor_of * jnp.repeat(jnp.exp(heights), extent[position] // shards_of).reshape((-1,) + (1,) * (len(extent) - 1 - position))
    return factor_of


def noise(key, shape, scale, bound, cuts=(), held_as=jnp.bfloat16):
    values = jax.random.normal(key, shape, jnp.float32) * scale
    if len(cuts) > 0:
        values = block_scale(key, shape, cuts, -0.22, 0.18) * values
    return jnp.clip(values, min=-bound, max=bound).astype(held_as)


def setup_inputs(seed: int = 0) -> dict:
    key_list = jax.random.split(jax.random.key(seed), 11)
    params = draw_params(jax.random.fold_in(key_list[10], 71), 0)
    angles_next = jnp.clip(jax.random.uniform(key_list[1], (TILES, 2), jnp.float32, -3.140625, 3.140625), -3.140625, 3.140625)
    angles_cur = jnp.clip(jax.random.uniform(key_list[2], (TILES, 2), jnp.float32, -3.140625, 3.140625), -3.140625, 3.140625)
    lists_next = draw_lists_next(jax.random.fold_in(key_list[10], 71), 0)
    lists_cur = draw_lists_cur(jax.random.fold_in(key_list[10], 71), 0)
    counts_next = draw_counts_next(jax.random.fold_in(key_list[10], 71), 0)
    counts_cur = draw_counts_cur(jax.random.fold_in(key_list[10], 71), 0)
    sends_next = touch_ends(jax.random.randint(key_list[7], (DEVICES, DEVICES, SLOTS), 0, GAUSS_DEV), jax.random.fold_in(key_list[7], 1), 0, GAUSS_DEV - 1).astype(jnp.int32)
    sends_cur = touch_ends(jax.random.randint(key_list[8], (DEVICES, DEVICES, SLOTS), 0, GAUSS_DEV), jax.random.fold_in(key_list[8], 1), 0, GAUSS_DEV - 1).astype(jnp.int32)
    cotangent = noise(key_list[9], (TILES, 3, TILE_PIX), 1.0, 6.0, ((0, 128),), jnp.float32)
    return dict(params=params, angles_next=angles_next, angles_cur=angles_cur, lists_next=lists_next, lists_cur=lists_cur, counts_next=counts_next, counts_cur=counts_cur, sends_next=sends_next, sends_cur=sends_cur, cotangent=cotangent)


precise = lax.Precision.HIGHEST


def sh_basis(angles):
    theta = angles[:, 0]
    azimuth = angles[:, 1]
    dir_x = jnp.sin(theta) * jnp.cos(azimuth)
    dir_y = jnp.sin(theta) * jnp.sin(azimuth)
    dir_z = jnp.cos(theta)
    sq_x = dir_x * dir_x
    sq_y = dir_y * dir_y
    sq_z = dir_z * dir_z
    terms = [
        0.28209479177387814 * jnp.ones_like(dir_x),
        -0.4886025119029199 * dir_y,
        0.4886025119029199 * dir_z,
        -0.4886025119029199 * dir_x,
        1.0925484305920792 * dir_x * dir_y,
        -1.0925484305920792 * dir_y * dir_z,
        0.31539156525252005 * (2.0 * sq_z - sq_x - sq_y),
        -1.0925484305920792 * dir_x * dir_z,
        0.5462742152960396 * (sq_x - sq_y),
        -0.5900435899266435 * dir_y * (3.0 * sq_x - sq_y),
        2.890611442640554 * dir_x * dir_y * dir_z,
        -0.4570457994644658 * dir_y * (4.0 * sq_z - sq_x - sq_y),
        0.3731763325901154 * dir_z * (2.0 * sq_z - 3.0 * sq_x - 3.0 * sq_y),
        -0.4570457994644658 * dir_x * (4.0 * sq_z - sq_x - sq_y),
        1.445305721320277 * dir_z * (sq_x - sq_y),
        -0.5900435899266435 * dir_x * (sq_x - 3.0 * sq_y),
    ]
    return jnp.stack(terms, 0)


def pixel_grid():
    pixels = jnp.arange(256)
    pos_x = (pixels % 16).astype(jnp.float32) + 0.5
    pos_y = (pixels // 16).astype(jnp.float32) + 0.5
    return pos_x, pos_y


def block_state(buffer, tile_lists, counts, harmonic_basis, offset):
    slot_ids = lax.dynamic_slice_in_dim(tile_lists, offset, 128, 1)
    members = buffer[:, slot_ids]
    live_mask = ((offset + jnp.arange(128))[None, :] < counts[:, None]).astype(jnp.float32)
    pos_x, pos_y = pixel_grid()
    off_x = pos_x[None, None, :] - members[0][:, :, None]
    off_y = pos_y[None, None, :] - members[1][:, :, None]
    con_a = members[2][:, :, None]
    con_b = members[3][:, :, None]
    con_c = members[4][:, :, None]
    exponent = -0.5 * (con_a * off_x * off_x + 2.0 * con_b * off_x * off_y + con_c * off_y * off_y)
    opacity = jax.nn.sigmoid(members[5])
    raw_alpha = opacity[:, :, None] * jnp.exp(exponent) * live_mask[:, :, None]
    alphas = jnp.minimum(raw_alpha, 0.99)
    unclamped = (raw_alpha < 0.99).astype(jnp.float32)
    tile_count = members.shape[1]
    harmonics = members[6:].reshape(3, 16, tile_count, 128)
    colors = 0.5 + jnp.einsum('cktj,kt->ctj', harmonics, harmonic_basis, precision=precise)
    return slot_ids, members, off_x, off_y, opacity, alphas, colors, unclamped


def weights_of(alphas, transmit):
    log_keep = jnp.log1p(-alphas)
    before = jnp.cumsum(log_keep, axis=1) - log_keep
    through = transmit[:, None, :] * jnp.exp(before)
    return log_keep, through, alphas * through


def render(buffer, tile_lists, counts, harmonic_basis, blocks):
    tile_count = tile_lists.shape[0]

    def advance(block_index, state_pair):
        transmit, pixel_color = state_pair
        parts = block_state(buffer, tile_lists, counts, harmonic_basis, block_index * 128)
        log_keep, through, weight = weights_of(parts[5], transmit)
        pixel_color = pixel_color + jnp.einsum('tjp,ctj->tcp', weight, parts[6], precision=precise)
        return transmit * jnp.exp(jnp.sum(log_keep, axis=1)), pixel_color

    initial = (jnp.ones((tile_count, 256), jnp.float32), jnp.zeros((tile_count, 3, 256), jnp.float32))
    return lax.fori_loop(0, blocks, advance, initial)[1]


def backprop(buffer, tile_lists, counts, harmonic_basis, blocks, upstream, final_color):
    tile_count = tile_lists.shape[0]
    upstream_total = jnp.sum(upstream * final_color, axis=1)

    def advance(block_index, state_triple):
        transmit, accum, slot_grads = state_triple
        slot_ids, members, off_x, off_y, opacity, alphas, colors, unclamped = block_state(
            buffer, tile_lists, counts, harmonic_basis, block_index * 128)
        log_keep, through, weight = weights_of(alphas, transmit)
        shade = jnp.einsum('tcp,ctj->tjp', upstream, colors, precision=precise)
        shaded = weight * shade
        behind = accum[:, None, :] + jnp.cumsum(shaded, axis=1)
        d_alpha = through * shade - (upstream_total[:, None, :] - behind) / (1.0 - alphas)
        d_colors = jnp.einsum('tcp,tjp->ctj', upstream, weight, precision=precise)
        d_power = d_alpha * alphas * unclamped
        con_a = members[2][:, :, None]
        con_b = members[3][:, :, None]
        con_c = members[4][:, :, None]
        grad_x = jnp.sum(d_power * (con_a * off_x + con_b * off_y), axis=2)
        grad_y = jnp.sum(d_power * (con_b * off_x + con_c * off_y), axis=2)
        grad_a = jnp.sum(-0.5 * off_x * off_x * d_power, axis=2)
        grad_b = jnp.sum(-off_x * off_y * d_power, axis=2)
        grad_c = jnp.sum(-0.5 * off_y * off_y * d_power, axis=2)
        grad_logit = jnp.sum(d_power, axis=2) * (1.0 - opacity)
        grad_harm = (d_colors[:, None, :, :] * harmonic_basis[None, :, :, None]).reshape(48, tile_count, 128)
        block_grads = jnp.concatenate(
            [jnp.stack([grad_x, grad_y, grad_a, grad_b, grad_c, grad_logit], 0), grad_harm], 0)
        slot_grads = slot_grads.at[:, slot_ids.reshape(-1)].add(block_grads.reshape(block_grads.shape[0], -1))
        return transmit * jnp.exp(jnp.sum(log_keep, axis=1)), accum + jnp.sum(shaded, axis=1), slot_grads

    initial = (jnp.ones((tile_count, 256), jnp.float32), jnp.zeros((tile_count, 256), jnp.float32),
               jnp.zeros(buffer.shape, jnp.float32))
    return lax.fori_loop(0, blocks, advance, initial)[2]


def slot_table(sends):
    devices = sends.shape[0]
    owners = (jnp.arange(devices).astype(jnp.int32) * GAUSS_DEV)[:, None, None]
    return jnp.transpose(sends + owners, (1, 0, 2)).reshape(devices, -1)


def reference(params, angles_next, angles_cur, lists_next, lists_cur, counts_next, counts_cur, sends_next, sends_cur, cotangent):
    devices = sends_next.shape[0]
    table_next = slot_table(sends_next)
    table_cur = slot_table(sends_cur)

    def forward_one(device):
        first_tile = (device * TILE_DEV).astype(jnp.int32)
        buffer = params[:, table_next[device]]
        tile_lists = lax.dynamic_slice_in_dim(lists_next, first_tile, TILE_DEV, 0)
        counts = lax.dynamic_slice_in_dim(counts_next, first_tile, TILE_DEV, 0)
        harmonic_basis = sh_basis(lax.dynamic_slice_in_dim(angles_next, first_tile, TILE_DEV, 0))
        return render(buffer, tile_lists, counts, harmonic_basis, BLOCKS)

    def backward_one(device):
        first_tile = (device * TILE_DEV).astype(jnp.int32)
        buffer = params[:, table_cur[device]]
        tile_lists = lax.dynamic_slice_in_dim(lists_cur, first_tile, TILE_DEV, 0)
        counts = lax.dynamic_slice_in_dim(counts_cur, first_tile, TILE_DEV, 0)
        harmonic_basis = sh_basis(lax.dynamic_slice_in_dim(angles_cur, first_tile, TILE_DEV, 0))
        upstream = lax.dynamic_slice_in_dim(cotangent, first_tile, TILE_DEV, 0)
        final_color = render(buffer, tile_lists, counts, harmonic_basis, BLOCKS)
        return backprop(buffer, tile_lists, counts, harmonic_basis, BLOCKS, upstream, final_color)

    device_ids = jnp.arange(devices).astype(jnp.int32)
    image_next = lax.map(forward_one, device_ids).reshape(devices * TILE_DEV, 3, 256)
    slot_grads = lax.map(backward_one, device_ids)
    flat = jnp.transpose(slot_grads, (1, 0, 2)).reshape(params.shape[0], -1)
    grads = jnp.zeros(params.shape, jnp.float32).at[:, table_cur.reshape(-1)].add(flat)
    return image_next, grads
```

```python
import jax
import jax.numpy as jnp
import numpy as np
from jax import lax
from jax.experimental import pallas as pl
from jax.experimental.pallas import tpu as pltpu
from jax.sharding import PartitionSpec as P

F32 = jnp.float32
BF16 = jnp.bfloat16
I32 = jnp.int32
AXES = ("gauss", "pix")
N_DEV = 128
N_PIX = 32
SLOTS = 32
GAUSS = 16384
HALF = 8192
ROWS = 54
LANES = 128
STEPS = 32
LOG2E = 1.4426950408889634
VMEM_LIMIT = 56 * 2**20


def iota(shape, dim):
    return lax.broadcasted_iota(I32, shape, dim)


def dot_nn(a, b):
    return lax.dot_general(a, b, (((1,), (0,)), ((), ())), preferred_element_type=F32)


def dot_nt(a, b):
    return lax.dot_general(a, b, (((1,), (1,)), ((), ())), preferred_element_type=F32)


def split2(x):
    high = x.astype(BF16)
    low = (x - high.astype(F32)).astype(BF16)
    return high, low


def split3(x):
    high = x.astype(BF16)
    rest = x - high.astype(F32)
    mid = rest.astype(BF16)
    low = (rest - mid.astype(F32)).astype(BF16)
    return high, mid, low


def pixel_tables():
    pixels = np.arange(256)
    qx = (pixels % 16) - 7.5
    qy = (pixels // 16) - 7.5
    mono = np.stack([np.ones(256), qx, qy, qx * qx, qx * qy, qy * qy], 0)
    power = np.zeros((32, 640), np.float32)
    for part in range(3):
        power[part * 6 : part * 6 + 6, :256] = mono
        for ch in range(3):
            power[18 + part * 3 + ch, 256 + 128 * ch : 384 + 128 * ch] = 1.0
    moments = np.zeros((16, 512), np.float32)
    moments[:6, :256] = mono
    moments[:6, 256:] = mono
    return jnp.asarray(power, BF16), jnp.asarray(moments, BF16)


def order_lists(lists_ref, turned, slots_ref):
    turned[:, 0:16] = lists_ref[...].astype(F32).T
    lane_group = iota((STEPS, LANES), 1) // 16
    out = jnp.zeros((STEPS, LANES), F32)
    for k in range(8):
        piece = pltpu.roll(turned[pl.ds(k, STEPS, stride=8), :], 16 * k, 1) if k else turned[pl.ds(0, STEPS, stride=8), :]
        out = jnp.where(lane_group == k, piece, out)
    slots_ref[...] = out.astype(I32)


def owner_onehot(slots_ref, hot_ref):
    rows = iota((N_DEV, LANES), 0)
    for q in range(STEPS):
        owner = slots_ref[q : q + 1, :] // SLOTS
        hot_ref[:, q * LANES : (q + 1) * LANES] = (rows == owner).astype(F32).astype(BF16)


def slot_tiles(slots_ref, hot_ref, mark_ref):
    rows = iota((SLOTS, LANES), 0)
    tile = (iota((SLOTS, LANES), 1) % 16).astype(F32)
    for q in range(STEPS):
        place = slots_ref[q : q + 1, :] % SLOTS
        mark_ref[:, q * LANES : (q + 1) * LANES] = jnp.where(rows == place, tile, 0.0).astype(BF16)
    return dot_nt(hot_ref[...], mark_ref[...])


def angle_message(tiles_next, tiles_cur, angles_next, angles_cur):
    tiles = jnp.concatenate([tiles_next, tiles_next, tiles_cur, tiles_cur], 1)
    region = iota((1, LANES), 1) // 32
    out = jnp.zeros((N_DEV, LANES), F32)
    for t in range(16):
        row = jnp.where(
            region < 2,
            jnp.where(region == 0, angles_next[t, 0], angles_next[t, 1]),
            jnp.where(region == 2, angles_cur[t, 0], angles_cur[t, 1]),
        )
        out = jnp.where(tiles == float(t), row, out)
    return out


def lists_kernel(lists_next, lists_cur, angles_next, angles_cur, msg, slots_next, slots_cur, hot_next, hot_cur, turned, mark):
    order_lists(lists_next, turned, slots_next)
    owner_onehot(slots_next, hot_next)
    tiles_next = slot_tiles(slots_next, hot_next, mark)
    order_lists(lists_cur, turned, slots_cur)
    owner_onehot(slots_cur, hot_cur)
    tiles_cur = slot_tiles(slots_cur, hot_cur, mark)
    msg[:, 0, :] = angle_message(tiles_next, tiles_cur, angles_next, angles_cur)


def sh_terms(theta, azimuth):
    sin_t = jnp.sin(theta)
    dir_x = sin_t * jnp.cos(azimuth)
    dir_y = sin_t * jnp.sin(azimuth)
    dir_z = jnp.cos(theta)
    sq_x = dir_x * dir_x
    sq_y = dir_y * dir_y
    sq_z = dir_z * dir_z
    return [
        0.28209479177387814 * jnp.ones_like(dir_x),
        -0.4886025119029199 * dir_y,
        0.4886025119029199 * dir_z,
        -0.4886025119029199 * dir_x,
        1.0925484305920792 * dir_x * dir_y,
        -1.0925484305920792 * dir_y * dir_z,
        0.31539156525252005 * (2.0 * sq_z - sq_x - sq_y),
        -1.0925484305920792 * dir_x * dir_z,
        0.5462742152960396 * (sq_x - sq_y),
        -0.5900435899266435 * dir_y * (3.0 * sq_x - sq_y),
        2.890611442640554 * dir_x * dir_y * dir_z,
        -0.4570457994644658 * dir_y * (4.0 * sq_z - sq_x - sq_y),
        0.3731763325901154 * dir_z * (2.0 * sq_z - 3.0 * sq_x - 3.0 * sq_y),
        -0.4570457994644658 * dir_x * (4.0 * sq_z - sq_x - sq_y),
        1.445305721320277 * dir_z * (sq_x - sq_y),
        -0.5900435899266435 * dir_x * (sq_x - 3.0 * sq_y),
    ]


def build_table(params, table):
    zeros = jnp.zeros((64 - ROWS, LANES), F32)

    def block(b, _):
        first = pl.multiple_of(b * LANES, LANES)
        both = jnp.concatenate(
            [params[:, pl.ds(first, LANES)], zeros, params[:, pl.ds(first + HALF, LANES)], zeros], 0
        )
        table[pl.ds(first, LANES), :] = both.T
        return 0

    lax.fori_loop(0, HALF // LANES, block, 0, unroll=4)


def gather_rows(index, table, rows, half_ref, turned):
    def pair(r2, _):
        for u in range(256):
            rows[u : u + 1, :] = table[pl.ds(index[r2 * 2 + u // 128, u % 128], 1), :]
        for k in range(2):
            r = r2 * 2 + k
            both = rows[k * 128 : k * 128 + 128, :].T
            upper = half_ref[pl.ds(r, 1), :] > 0.5
            turned[pl.ds(pl.multiple_of(r * 64, 64), 64), :] = jnp.where(upper, both[64:], both[:64])
        return 0

    lax.fori_loop(0, SLOTS // 2, pair, 0)


def split_index(sends_ref, row_ref, half_ref):
    turned = sends_ref[...].astype(F32).T
    upper = turned >= float(HALF)
    half_ref[...] = upper.astype(F32)
    row_ref[...] = jnp.where(upper, turned - float(HALF), turned).astype(I32)


def color_rows(basis, turned, color):
    def one(r, _):
        terms = basis[pl.ds(r, 16, stride=32), :]
        for ch in range(3):
            start = r * 64 + 6 + 16 * ch
            color[pl.ds(ch * 32 + r, 1), :] = 0.5 + jnp.sum(terms * turned[pl.ds(start, 16), :], axis=0, keepdims=True)
        return 0

    lax.fori_loop(0, SLOTS, one, 0, unroll=4)


def owner_message(turned, color, msg):
    geo = [turned[pl.ds(v, 32, stride=64), :] for v in range(6)]
    msg[:, 0, 0:128] = jnp.concatenate(geo[0:4], 0).T
    msg[:, 0, 128:256] = jnp.concatenate([geo[4], geo[5], color[0:32], color[32:64]], 0).T
    last = color[64:96]
    msg[:, 0, 256:384] = jnp.concatenate([last, last, last, last], 0).T


def owner_kernel(
    params, sends_next, sends_cur, angles, msg_next, msg_cur, basis_cur,
    table, rows, turned, row_v, half_next, half_cur, row_next, row_cur, basis_next, color, sem,
):
    split_index(sends_next, row_v, half_next)
    copy = pltpu.make_async_copy(row_v, row_next, sem)
    copy.start()
    copy.wait()
    split_index(sends_cur, row_v, half_cur)
    copy = pltpu.make_async_copy(row_v, row_cur, sem)
    copy.start()
    copy.wait()
    build_table(params, table)
    seen = angles[:, 0, :].T
    for k, term in enumerate(sh_terms(seen[0:32], seen[32:64])):
        basis_next[k * 32 : k * 32 + 32, :] = term
    for k, term in enumerate(sh_terms(seen[64:96], seen[96:128])):
        basis_cur[k * 32 : k * 32 + 32, :] = term
    gather_rows(row_cur, table, rows, half_cur, turned)
    color_rows(basis_cur, turned, color)
    owner_message(turned, color, msg_cur)
    gather_rows(row_next, table, rows, half_next, turned)
    color_rows(basis_next, turned, color)
    owner_message(turned, color, msg_next)


def entries_in_order(got, hot, slots, split, entry):
    for g, size in ((0, 128), (1, 128), (2, 32)):
        parts = split3(got[:, 0, g * 128 : g * 128 + 128].T[0:size])
        for k in range(3):
            split[g * 128 : g * 128 + size, k * 128 : k * 128 + 128] = parts[k]
    rows = iota((SLOTS, LANES), 0)

    def step(q, _):
        cols = hot[:, pl.ds(pl.multiple_of(q * LANES, LANES), LANES)]
        picked = dot_nn(split[...], jnp.concatenate([cols, cols, cols], 0))
        here = rows == slots[pl.ds(q, 1), :] % SLOTS
        for v in range(9):
            kept = jnp.where(here, picked[v * 32 : v * 32 + 32], 0.0)
            entry[pl.ds(v * 32 + q, 1), :] = jnp.sum(kept, axis=0, keepdims=True)
        return 0

    lax.fori_loop(0, STEPS, step, 0, unroll=2)


def power_factors(entry, counts, factor):
    x = entry[0:32] - 8.0
    y = entry[32:64] - 8.0
    con_a = entry[64:96]
    con_b = entry[96:128]
    con_c = entry[128:160]
    logit = entry[160:192]
    position = iota((STEPS, LANES), 0) * 8 + iota((STEPS, LANES), 1) // 16
    tile = iota((STEPS, LANES), 1) % 16
    count = jnp.zeros((STEPS, LANES), I32)
    for t in range(16):
        count = jnp.where(tile == t, counts[t], count)
    live = position < count
    lin_x = con_a * x + con_b * y
    lin_y = con_b * x + con_c * y
    const = -0.5 * (x * lin_x + y * lin_y) - jnp.log(1.0 + jnp.exp(-logit))
    factors = [const, lin_x, lin_y, -0.5 * con_a, -con_b, -0.5 * con_c]
    for k, value in enumerate(factors):
        value = jnp.where(live, value * LOG2E, -1000.0 if k == 0 else 0.0)
        for p, part in enumerate(split3(value)):
            row = (p * 6 + k) * 32
            factor[row : row + 32, :] = part.astype(F32)
    for ch in range(3):
        for p, part in enumerate(split3(entry[192 + ch * 32 : 224 + ch * 32])):
            row = (18 + p * 3 + ch) * 32
            factor[row : row + 32, :] = part.astype(F32)
    factor[27 * 32 : 32 * 32, :] = jnp.zeros((5 * 32, LANES), F32)


def alphas_and_colors(factor, power, alpha, shade):
    def step(q, _):
        first = pl.multiple_of(q * LANES, LANES)
        left = factor[pl.ds(q, 32, stride=32), :].T.astype(BF16)
        out = dot_nn(left, power[...])
        alpha[pl.ds(first, LANES), :] = jnp.minimum(jnp.exp2(out[:, 0:256]), 0.99)
        shade[pl.ds(first, LANES), :] = out[:, 256:640]
        return 0

    lax.fori_loop(0, STEPS, step, 0, unroll=2)


def composite(alpha, shade, image):
    one = jnp.ones((16, LANES), F32)
    zero = jnp.zeros((16, LANES), F32)

    def step(q, state):
        through = list(state[0:2])
        total = list(state[2:8])
        for k in range(8):
            row = pl.ds(pl.multiple_of(q * LANES + k * 16, 16), 16)
            colors = [shade[row, ch * 128 : ch * 128 + 128] for ch in range(3)]
            for h in range(2):
                weight = alpha[row, h * 128 : h * 128 + 128] * through[h]
                through[h] = through[h] - weight
                for ch in range(3):
                    total[ch * 2 + h] = total[ch * 2 + h] + weight * colors[ch]
        return tuple(through + total)

    state = lax.fori_loop(0, STEPS, step, (one, one) + (zero,) * 6)
    for ch in range(3):
        for h in range(2):
            image[ch, :, h * 128 : h * 128 + 128] = state[2 + ch * 2 + h]


def weights_forward(alpha, weights):
    one = jnp.ones((16, LANES), F32)

    def step(q, through):
        through = list(through)
        for k in range(8):
            row = pl.ds(pl.multiple_of(q * LANES + k * 16, 16), 16)
            for h in range(2):
                weight = alpha[row, h * 128 : h * 128 + 128] * through[h]
                through[h] = through[h] - weight
                weights[row, h * 128 : h * 128 + 128] = weight
        return tuple(through)

    lax.fori_loop(0, STEPS, step, (one, one))


def backward(alpha, shade, weights, cot, pull, held):
    up = [cot[ch, :, h * 128 : h * 128 + 128] for ch in range(3) for h in range(2)]
    zero = jnp.zeros((16, LANES), F32)

    def step(s, behind):
        behind = list(behind)
        q = STEPS - 1 - s
        for k in range(7, -1, -1):
            row = pl.ds(pl.multiple_of(q * LANES + k * 16, 16), 16)
            colors = [shade[row, ch * 128 : ch * 128 + 128] for ch in range(3)]
            for h in range(2):
                opaque = alpha[row, h * 128 : h * 128 + 128]
                weight = weights[row, h * 128 : h * 128 + 128]
                value = up[h] * colors[0] + up[2 + h] * colors[1] + up[4 + h] * colors[2]
                ahead = value - behind[h]
                behind[h] = behind[h] + opaque * ahead
                pulled = jnp.where(opaque < 0.99, weight * ahead, 0.0)
                high, low = split2(pulled)
                pull[row, h * 128 : h * 128 + 128] = high
                pull[row, 256 + h * 128 : 384 + h * 128] = low
                high, low = split2(weight)
                held[row, h * 128 : h * 128 + 128] = high
                held[row, 256 + h * 128 : 384 + h * 128] = low
        return tuple(behind)

    lax.fori_loop(0, STEPS, step, (zero, zero))


def pixel_sums(pull, held, moments, cot, cots, sums):
    flat = cot[...].reshape(48, 256)
    high, low = split2(flat)
    cots[:, 0:256] = high
    cots[:, 256:512] = high
    cots[:, 512:768] = low
    own = iota((16, LANES), 0) == iota((16, LANES), 1) % 16

    def step(q, _):
        row = pl.ds(pl.multiple_of(q * LANES, LANES), LANES)
        moment = dot_nt(moments[...], pull[row, :])
        for v in range(6):
            sums[pl.ds(v * 32 + q, 1), :] = moment[v : v + 1]
        both = held[row, :]
        spread = dot_nt(cots[...], jnp.concatenate([both, both[:, 0:256]], 1))
        for ch in range(3):
            kept = jnp.where(own, spread[ch * 16 : ch * 16 + 16], 0.0)
            sums[pl.ds((6 + ch) * 32 + q, 1), :] = jnp.sum(kept, axis=0, keepdims=True)
        return 0

    lax.fori_loop(0, STEPS, step, 0, unroll=2)


def entry_gradients(entry, sums, grad):
    x = entry[0:32] - 8.0
    y = entry[32:64] - 8.0
    con_a = entry[64:96]
    con_b = entry[96:128]
    con_c = entry[128:160]
    fade = jnp.exp(-entry[160:192])
    s_0 = sums[0:32]
    s_x = sums[32:64]
    s_y = sums[64:96]
    d_x = s_x - x * s_0
    d_y = s_y - y * s_0
    d_xx = sums[96:128] - x * (s_x + d_x)
    d_xy = sums[128:160] - x * s_y - y * d_x
    d_yy = sums[160:192] - y * (s_y + d_y)
    values = [
        con_a * d_x + con_b * d_y,
        con_b * d_x + con_c * d_y,
        -0.5 * d_xx,
        -d_xy,
        -0.5 * d_yy,
        s_0 * (fade / (1.0 + fade)),
        sums[192:224],
        sums[224:256],
        sums[256:288],
    ]
    for v, value in enumerate(values):
        grad[v * 32 : v * 32 + 32, :] = value


def slots_in_order(grad, hot, slots, spread, msg):
    rows = iota((SLOTS, LANES), 0)

    def step(q, _):
        first = pl.multiple_of(q * LANES, LANES)
        here = rows == slots[pl.ds(q, 1), :] % SLOTS
        for v in range(9):
            value = grad[pl.ds(v * 32 + q, 1), :]
            high, low = split2(jnp.where(here, value, 0.0))
            spread[v * 32 : v * 32 + 32, pl.ds(first, LANES)] = high
            spread[288 + v * 32 : 320 + v * 32, pl.ds(first, LANES)] = low
        return 0

    lax.fori_loop(0, STEPS, step, 0, unroll=2)
    for g, size in ((0, 128), (1, 128), (2, 32)):
        high = dot_nt(hot[...], spread[g * 128 : g * 128 + size, :])
        low = dot_nt(hot[...], spread[288 + g * 128 : 288 + g * 128 + size, :])
        msg[:, 0, g * 128 : g * 128 + size] = high + low


def render_kernel(
    got_next, got_cur, hot_next, hot_cur, slots_next, slots_cur, counts_next, counts_cur, cot, power, moments,
    image, msg,
    split, entry, factor, alpha, shade, weights, pull, held, cots, sums, grad, spread,
):
    entries_in_order(got_cur, hot_cur, slots_cur, split, entry)
    power_factors(entry, counts_cur, factor)
    alphas_and_colors(factor, power, alpha, shade)
    weights_forward(alpha, weights)
    backward(alpha, shade, weights, cot, pull, held)
    pixel_sums(pull, held, moments, cot, cots, sums)
    entry_gradients(entry, sums, grad)
    slots_in_order(grad, hot_cur, slots_cur, spread, msg)
    msg[:, 0, 288:384] = jnp.zeros((N_DEV, 96), F32)
    entries_in_order(got_next, hot_next, slots_next, split, entry)
    power_factors(entry, counts_next, factor)
    alphas_and_colors(factor, power, alpha, shade)
    composite(alpha, shade, image)


def scatter_kernel(got, basis, sends, grads, turned, row_v, half, row_s, total, piece, rows, sem):
    split_index(sends, row_v, half)
    copy = pltpu.make_async_copy(row_v, row_s, sem)
    copy.start()
    for g in range(3):
        turned[g * 128 : g * 128 + 128, :] = got[:, 0, g * 128 : g * 128 + 128].T

    def clear(b, _):
        total[pl.ds(pl.multiple_of(b * 256, 256), 256), :] = jnp.zeros((256, LANES), F32)
        return 0

    lax.fori_loop(0, HALF // 256, clear, 0)
    piece[48:64, :] = jnp.zeros((16, LANES), F32)
    same_group = iota((LANES, LANES), 0) // 16 == iota((LANES, LANES), 1) // 16
    copy.wait()

    def slot(r, _):
        piece[0:6, :] = turned[pl.ds(r, 8, stride=32), :][0:6]
        terms = basis[pl.ds(r, 16, stride=32), :]
        for ch in range(3):
            piece[6 + 16 * ch : 22 + 16 * ch, :] = terms * turned[pl.ds((6 + ch) * 32 + r, 1), :]
        upper = half[pl.ds(r, 1), :] > 0.5
        values = piece[...]
        both = jnp.concatenate([jnp.where(upper, 0.0, values), jnp.where(upper, values, 0.0)], 0)
        high, low = split2(both)
        name = jnp.broadcast_to(row_v[pl.ds(r, 1), :].astype(F32), (LANES, LANES))
        same = jnp.logical_and(name == name.T, same_group).astype(F32).astype(BF16)
        rows[...] = dot_nt(jnp.concatenate([same, same], 1), jnp.concatenate([high, low], 1))
        for g in range(8):
            places = [row_s[r, g * 16 + u] for u in range(16)]
            olds = [total[pl.ds(places[u], 1), :] for u in range(16)]
            for u in range(16):
                total[pl.ds(places[u], 1), :] = olds[u] + rows[g * 16 + u : g * 16 + u + 1, :]
        return 0

    lax.fori_loop(0, SLOTS, slot, 0)

    def block(b, _):
        first = pl.multiple_of(b * LANES, LANES)
        both = total[pl.ds(first, LANES), :].T
        grads[:, pl.ds(first, LANES)] = both[0:ROWS]
        grads[:, pl.ds(first + HALF, LANES)] = both[64 : 64 + ROWS]
        return 0

    lax.fori_loop(0, HALF // LANES, block, 0, unroll=4)


VM = pl.BlockSpec(memory_space=pltpu.VMEM)
SM = pl.BlockSpec(memory_space=pltpu.SMEM)
PARAMS = pltpu.CompilerParams(vmem_limit_bytes=VMEM_LIMIT)


def shape(dims, dtype=F32):
    return jax.ShapeDtypeStruct(dims, dtype)


def exchange(x):
    return lax.all_to_all(x, AXES, split_axis=0, concat_axis=0, tiled=True)


def body(params, angles_next, angles_cur, lists_next, lists_cur, counts_next, counts_cur, sends_next, sends_cur, cotangent):
    power, moments = pixel_tables()
    hots = (N_DEV, 4096)
    dense = (STEPS, LANES)
    msg, slots_next, slots_cur, hot_next, hot_cur = pl.pallas_call(
        lists_kernel,
        out_shape=(shape((N_DEV, 1, 128)), shape(dense, I32), shape(dense, I32), shape(hots, BF16), shape(hots, BF16)),
        in_specs=[VM, VM, SM, SM],
        out_specs=(VM,) * 5,
        scratch_shapes=[pltpu.VMEM((256, LANES), F32), pltpu.VMEM((SLOTS, 4096), BF16)],
        compiler_params=PARAMS,
        name="lists",
    )(lists_next, lists_cur, angles_next, angles_cur)
    angles = exchange(msg)
    msg_next, msg_cur, basis = pl.pallas_call(
        owner_kernel,
        out_shape=(shape((N_DEV, 1, 384)), shape((N_DEV, 1, 384)), shape((512, LANES))),
        in_specs=[VM, VM, VM, VM],
        out_specs=(VM,) * 3,
        scratch_shapes=[
            pltpu.VMEM((HALF, LANES), F32),
            pltpu.VMEM((256, LANES), F32),
            pltpu.VMEM((SLOTS * 64, LANES), F32),
            pltpu.VMEM(dense, I32),
            pltpu.VMEM(dense, F32),
            pltpu.VMEM(dense, F32),
            pltpu.SMEM(dense, I32),
            pltpu.SMEM(dense, I32),
            pltpu.VMEM((512, LANES), F32),
            pltpu.VMEM((96, LANES), F32),
            pltpu.SemaphoreType.DMA,
        ],
        compiler_params=PARAMS,
        name="owner",
    )(params, sends_next[0], sends_cur[0], angles)
    got_cur = exchange(msg_cur)
    got_next = exchange(msg_next)
    image, msg = pl.pallas_call(
        render_kernel,
        out_shape=(shape((3, 16, 256)), shape((N_DEV, 1, 384))),
        in_specs=[VM] * 6 + [SM, SM] + [VM] * 3,
        out_specs=(VM,) * 2,
        scratch_shapes=[
            pltpu.VMEM((288, 384), BF16),
            pltpu.VMEM((288, LANES), F32),
            pltpu.VMEM((1024, LANES), F32),
            pltpu.VMEM((4096, 256), F32),
            pltpu.VMEM((4096, 384), F32),
            pltpu.VMEM((4096, 256), F32),
            pltpu.VMEM((4096, 512), BF16),
            pltpu.VMEM((4096, 512), BF16),
            pltpu.VMEM((48, 768), BF16),
            pltpu.VMEM((288, LANES), F32),
            pltpu.VMEM((288, LANES), F32),
            pltpu.VMEM((576, 4096), BF16),
        ],
        compiler_params=PARAMS,
        name="render",
    )(got_next, got_cur, hot_next, hot_cur, slots_next, slots_cur, counts_next, counts_cur,
      jnp.transpose(cotangent, (1, 0, 2)), power, moments)
    got = exchange(msg)
    grads = pl.pallas_call(
        scatter_kernel,
        out_shape=shape((ROWS, GAUSS)),
        in_specs=[VM] * 3,
        out_specs=VM,
        scratch_shapes=[
            pltpu.VMEM((384, LANES), F32),
            pltpu.VMEM(dense, I32),
            pltpu.VMEM(dense, F32),
            pltpu.SMEM(dense, I32),
            pltpu.VMEM((HALF, LANES), F32),
            pltpu.VMEM((64, LANES), F32),
            pltpu.VMEM((LANES, LANES), F32),
            pltpu.SemaphoreType.DMA,
        ],
        compiler_params=PARAMS,
        name="scatter",
    )(got, basis, sends_cur[0])
    return jnp.transpose(image, (1, 0, 2)), grads


def solution(mesh):
    both = ("gauss", "pix")
    placed = (
        P(None, both),
        P(both, None),
        P(both, None),
        P(both, None),
        P(both, None),
        P(both),
        P(both),
        P(both, None, None),
        P(both, None, None),
        P(both, None, None),
    )
    return jax.shard_map(
        body,
        mesh=mesh,
        in_specs=placed,
        out_specs=(P(both, None, None), P(None, both)),
        check_vma=False,
    )
```

```python
import jax
import jax.numpy as jnp
import numpy as np
from jax import lax
from jax.experimental import pallas as pl
from jax.experimental.pallas import tpu as pltpu
from jax.sharding import PartitionSpec as P

F32 = jnp.float32
BF16 = jnp.bfloat16
I32 = jnp.int32
MESH = pl.DeviceIdType.MESH
N_DEV = 128
N_PIX = 32
SLOTS = 32
GAUSS = 16384
HALF = 8192
CHUNKS = 4
ROWS = 54
LANES = 128
STEPS = 32
LOG2E = 1.4426950408889634
VMEM_LIMIT = 56 * 2**20


def iota(shape, dim):
    return lax.broadcasted_iota(I32, shape, dim)


def dot_nn(a, b):
    return lax.dot_general(a, b, (((1,), (0,)), ((), ())), preferred_element_type=F32)


def dot_nt(a, b):
    return lax.dot_general(a, b, (((1,), (1,)), ((), ())), preferred_element_type=F32)


def split2(x):
    high = x.astype(BF16)
    low = (x - high.astype(F32)).astype(BF16)
    return high, low


def split3(x):
    high = x.astype(BF16)
    rest = x - high.astype(F32)
    mid = rest.astype(BF16)
    low = (rest - mid.astype(F32)).astype(BF16)
    return high, mid, low


def pixel_tables():
    pixels = np.arange(256)
    qx = (pixels % 16) - 7.5
    qy = (pixels // 16) - 7.5
    mono = np.stack([np.ones(256), qx, qy, qx * qx, qx * qy, qy * qy], 0)
    power = np.zeros((32, 640), np.float32)
    for part in range(3):
        power[part * 6 : part * 6 + 6, :256] = mono
        for ch in range(3):
            power[18 + part * 3 + ch, 256 + 128 * ch : 384 + 128 * ch] = 1.0
    moments = np.zeros((16, 512), np.float32)
    moments[:6, :256] = mono
    moments[:6, 256:] = mono
    return jnp.asarray(power, BF16), jnp.asarray(moments, BF16)


def order_lists(lists_ref, turned, slots_ref):
    turned[0:256, 0:16] = lists_ref[...].T
    lane_group = iota((STEPS, LANES), 1) // 16
    out = jnp.zeros((STEPS, LANES), I32)
    for k in range(8):
        piece = pltpu.roll(turned[pl.ds(k, STEPS, stride=8), :], 16 * k, 1) if k else turned[pl.ds(0, STEPS, stride=8), :]
        out = jnp.where(lane_group == k, piece, out)
    slots_ref[...] = out


def owner_onehot(slots_ref, hot_ref):
    rows = iota((N_DEV, LANES), 0)
    for q in range(STEPS):
        owner = slots_ref[q : q + 1, :] // SLOTS
        hot_ref[:, q * LANES : (q + 1) * LANES] = (rows == owner).astype(F32).astype(BF16)


def slot_tiles(slots_ref, hot_ref, mark_ref):
    rows = iota((SLOTS, LANES), 0)
    tile = (iota((SLOTS, LANES), 1) % 16).astype(F32)
    for q in range(STEPS):
        place = slots_ref[q : q + 1, :] % SLOTS
        mark_ref[:, q * LANES : (q + 1) * LANES] = jnp.where(rows == place, tile, 0.0).astype(BF16)
    return dot_nt(hot_ref[...], mark_ref[...])


def angle_message(tiles_next, tiles_cur, angles_next, angles_cur):
    tiles = jnp.concatenate([tiles_next, tiles_next, tiles_cur, tiles_cur], 1)
    region = iota((1, LANES), 1) // 32
    out = jnp.zeros((N_DEV, LANES), F32)
    for t in range(16):
        row = jnp.where(
            region < 2,
            jnp.where(region == 0, angles_next[t, 0], angles_next[t, 1]),
            jnp.where(region == 2, angles_cur[t, 0], angles_cur[t, 1]),
        )
        out = jnp.where(tiles == float(t), row, out)
    return out


def sh_terms(theta, azimuth):
    sin_t = jnp.sin(theta)
    dir_x = sin_t * jnp.cos(azimuth)
    dir_y = sin_t * jnp.sin(azimuth)
    dir_z = jnp.cos(theta)
    sq_x = dir_x * dir_x
    sq_y = dir_y * dir_y
    sq_z = dir_z * dir_z
    return [
        0.28209479177387814 * jnp.ones_like(dir_x),
        -0.4886025119029199 * dir_y,
        0.4886025119029199 * dir_z,
        -0.4886025119029199 * dir_x,
        1.0925484305920792 * dir_x * dir_y,
        -1.0925484305920792 * dir_y * dir_z,
        0.31539156525252005 * (2.0 * sq_z - sq_x - sq_y),
        -1.0925484305920792 * dir_x * dir_z,
        0.5462742152960396 * (sq_x - sq_y),
        -0.5900435899266435 * dir_y * (3.0 * sq_x - sq_y),
        2.890611442640554 * dir_x * dir_y * dir_z,
        -0.4570457994644658 * dir_y * (4.0 * sq_z - sq_x - sq_y),
        0.3731763325901154 * dir_z * (2.0 * sq_z - 3.0 * sq_x - 3.0 * sq_y),
        -0.4570457994644658 * dir_x * (4.0 * sq_z - sq_x - sq_y),
        1.445305721320277 * dir_z * (sq_x - sq_y),
        -0.5900435899266435 * dir_x * (sq_x - 3.0 * sq_y),
    ]


def param_copies(params, held, sems):
    width = HALF // CHUNKS
    out = []
    for c in range(CHUNKS):
        for k in range(2):
            cols = pl.ds(k * HALF + c * width, width)
            out.append(pltpu.make_async_copy(params.at[:, cols], held.at[:, cols], sems.at[c * 2 + k]))
    return out


def build_table(copies, params, table):
    zeros = jnp.zeros((64 - ROWS, LANES), F32)
    blocks = HALF // LANES // CHUNKS

    for c in range(CHUNKS):
        copies[c * 2].wait()
        copies[c * 2 + 1].wait()

        def block(b, _):
            first = pl.multiple_of((c * blocks + b) * LANES, LANES)
            both = jnp.concatenate(
                [params[:, pl.ds(first, LANES)], zeros, params[:, pl.ds(first + HALF, LANES)], zeros], 0
            )
            table[pl.ds(first, LANES), :] = both.T
            return 0

        lax.fori_loop(0, blocks, block, 0, unroll=8)


def gather_rows(index, table, rows, half_ref, turned):
    def pair(r2, _):
        for u in range(256):
            rows[u : u + 1, :] = table[pl.ds(index[r2 * 2 + u // 128, u % 128], 1), :]
        for k in range(2):
            r = r2 * 2 + k
            both = rows[k * 128 : k * 128 + 128, :].T
            upper = half_ref[pl.ds(r, 1), :] > 0
            turned[pl.ds(pl.multiple_of(r * 64, 64), 64), :] = jnp.where(upper, both[64:], both[:64])
        return 0

    lax.fori_loop(0, SLOTS // 2, pair, 0)


def split_index(sends_ref, row_ref, half_ref):
    turned = sends_ref[...].T
    half_ref[...] = turned // HALF
    row_ref[...] = turned % HALF


def color_rows(basis, turned, color):
    def one(r, _):
        terms = basis[pl.ds(r, 16, stride=32), :]
        for ch in range(3):
            start = r * 64 + 6 + 16 * ch
            color[pl.ds(ch * 32 + r, 1), :] = 0.5 + jnp.sum(terms * turned[pl.ds(start, 16), :], axis=0, keepdims=True)
        return 0

    lax.fori_loop(0, SLOTS, one, 0, unroll=4)


def owner_message(turned, color, msg):
    geo = [turned[pl.ds(v, 32, stride=64), :] for v in range(6)]
    msg[:, 0, 0:128] = jnp.concatenate(geo[0:4], 0).T
    msg[:, 0, 128:256] = jnp.concatenate([geo[4], geo[5], color[0:32], color[32:64]], 0).T
    last = color[64:96]
    msg[:, 0, 256:384] = jnp.concatenate([last, last, last, last], 0).T


def entries_in_order(got, hot, slots, split, entry):
    for g, size in ((0, 128), (1, 128), (2, 32)):
        parts = split3(got[:, 0, g * 128 : g * 128 + 128].T[0:size])
        for k in range(3):
            split[g * 128 : g * 128 + size, k * 128 : k * 128 + 128] = parts[k]
    rows = iota((SLOTS, LANES), 0)

    def step(q, _):
        cols = hot[:, pl.ds(pl.multiple_of(q * LANES, LANES), LANES)]
        picked = dot_nn(split[...], jnp.concatenate([cols, cols, cols], 0))
        here = rows == slots[pl.ds(q, 1), :] % SLOTS
        for v in range(9):
            kept = jnp.where(here, picked[v * 32 : v * 32 + 32], 0.0)
            entry[pl.ds(v * 32 + q, 1), :] = jnp.sum(kept, axis=0, keepdims=True)
        return 0

    lax.fori_loop(0, STEPS, step, 0, unroll=2)


def power_factors(entry, counts, factor):
    x = entry[0:32] - 8.0
    y = entry[32:64] - 8.0
    con_a = entry[64:96]
    con_b = entry[96:128]
    con_c = entry[128:160]
    logit = entry[160:192]
    position = iota((STEPS, LANES), 0) * 8 + iota((STEPS, LANES), 1) // 16
    tile = iota((STEPS, LANES), 1) % 16
    count = jnp.zeros((STEPS, LANES), I32)
    for t in range(16):
        count = jnp.where(tile == t, counts[t], count)
    live = position < count
    lin_x = con_a * x + con_b * y
    lin_y = con_b * x + con_c * y
    const = -0.5 * (x * lin_x + y * lin_y) - jnp.log(1.0 + jnp.exp(-logit))
    factors = [const, lin_x, lin_y, -0.5 * con_a, -con_b, -0.5 * con_c]
    for k, value in enumerate(factors):
        value = jnp.where(live, value * LOG2E, -1000.0 if k == 0 else 0.0)
        for p, part in enumerate(split3(value)):
            row = (p * 6 + k) * 32
            factor[row : row + 32, :] = part.astype(F32)
    for ch in range(3):
        for p, part in enumerate(split3(entry[192 + ch * 32 : 224 + ch * 32])):
            row = (18 + p * 3 + ch) * 32
            factor[row : row + 32, :] = part.astype(F32)
    factor[27 * 32 : 32 * 32, :] = jnp.zeros((5 * 32, LANES), F32)


def alphas_and_colors(factor, power, alpha, shade):
    def step(q, _):
        first = pl.multiple_of(q * LANES, LANES)
        left = factor[pl.ds(q, 32, stride=32), :].T.astype(BF16)
        out = dot_nn(left, power[...])
        alpha[pl.ds(first, LANES), :] = jnp.minimum(jnp.exp2(out[:, 0:256]), 0.99)
        shade[pl.ds(first, LANES), :] = out[:, 256:640]
        return 0

    lax.fori_loop(0, STEPS, step, 0, unroll=2)


def composite(alpha, shade, image):
    one = jnp.ones((16, LANES), F32)
    zero = jnp.zeros((16, LANES), F32)

    def step(q, state):
        through = list(state[0:2])
        total = list(state[2:8])
        for k in range(8):
            row = pl.ds(pl.multiple_of(q * LANES + k * 16, 16), 16)
            colors = [shade[row, ch * 128 : ch * 128 + 128] for ch in range(3)]
            for h in range(2):
                weight = alpha[row, h * 128 : h * 128 + 128] * through[h]
                through[h] = through[h] - weight
                for ch in range(3):
                    total[ch * 2 + h] = total[ch * 2 + h] + weight * colors[ch]
        return tuple(through + total)

    state = lax.fori_loop(0, STEPS, step, (one, one) + (zero,) * 6)
    for ch in range(3):
        for h in range(2):
            image[ch, :, h * 128 : h * 128 + 128] = state[2 + ch * 2 + h]


def weights_forward(alpha, weights):
    one = jnp.ones((16, LANES), F32)

    def step(q, through):
        through = list(through)
        for k in range(8):
            row = pl.ds(pl.multiple_of(q * LANES + k * 16, 16), 16)
            for h in range(2):
                weight = alpha[row, h * 128 : h * 128 + 128] * through[h]
                through[h] = through[h] - weight
                weights[row, h * 128 : h * 128 + 128] = weight
        return tuple(through)

    lax.fori_loop(0, STEPS, step, (one, one))


def backward(alpha, shade, weights, cot, pull, held):
    up = [cot[ch, :, h * 128 : h * 128 + 128] for ch in range(3) for h in range(2)]
    zero = jnp.zeros((16, LANES), F32)

    def step(s, behind):
        behind = list(behind)
        q = STEPS - 1 - s
        for k in range(7, -1, -1):
            row = pl.ds(pl.multiple_of(q * LANES + k * 16, 16), 16)
            colors = [shade[row, ch * 128 : ch * 128 + 128] for ch in range(3)]
            for h in range(2):
                opaque = alpha[row, h * 128 : h * 128 + 128]
                weight = weights[row, h * 128 : h * 128 + 128]
                value = up[h] * colors[0] + up[2 + h] * colors[1] + up[4 + h] * colors[2]
                ahead = value - behind[h]
                behind[h] = behind[h] + opaque * ahead
                pulled = jnp.where(opaque < 0.99, weight * ahead, 0.0)
                high, low = split2(pulled)
                pull[row, h * 128 : h * 128 + 128] = high
                pull[row, 256 + h * 128 : 384 + h * 128] = low
                high, low = split2(weight)
                held[row, h * 128 : h * 128 + 128] = high
                held[row, 256 + h * 128 : 384 + h * 128] = low
        return tuple(behind)

    lax.fori_loop(0, STEPS, step, (zero, zero))


def pixel_sums(pull, held, moments, cot, cots, sums):
    flat = cot[...].reshape(48, 256)
    high, low = split2(flat)
    cots[:, 0:256] = high
    cots[:, 256:512] = high
    cots[:, 512:768] = low
    own = iota((16, LANES), 0) == iota((16, LANES), 1) % 16

    def step(q, _):
        row = pl.ds(pl.multiple_of(q * LANES, LANES), LANES)
        moment = dot_nt(moments[...], pull[row, :])
        for v in range(6):
            sums[pl.ds(v * 32 + q, 1), :] = moment[v : v + 1]
        both = held[row, :]
        spread = dot_nt(cots[...], jnp.concatenate([both, both[:, 0:256]], 1))
        for ch in range(3):
            kept = jnp.where(own, spread[ch * 16 : ch * 16 + 16], 0.0)
            sums[pl.ds((6 + ch) * 32 + q, 1), :] = jnp.sum(kept, axis=0, keepdims=True)
        return 0

    lax.fori_loop(0, STEPS, step, 0, unroll=2)


def entry_gradients(entry, sums, grad):
    x = entry[0:32] - 8.0
    y = entry[32:64] - 8.0
    con_a = entry[64:96]
    con_b = entry[96:128]
    con_c = entry[128:160]
    fade = jnp.exp(-entry[160:192])
    s_0 = sums[0:32]
    s_x = sums[32:64]
    s_y = sums[64:96]
    d_x = s_x - x * s_0
    d_y = s_y - y * s_0
    d_xx = sums[96:128] - x * (s_x + d_x)
    d_xy = sums[128:160] - x * s_y - y * d_x
    d_yy = sums[160:192] - y * (s_y + d_y)
    values = [
        con_a * d_x + con_b * d_y,
        con_b * d_x + con_c * d_y,
        -0.5 * d_xx,
        -d_xy,
        -0.5 * d_yy,
        s_0 * (fade / (1.0 + fade)),
        sums[192:224],
        sums[224:256],
        sums[256:288],
    ]
    for v, value in enumerate(values):
        grad[v * 32 : v * 32 + 32, :] = value


def slots_in_order(grad, hot, slots, spread, msg):
    rows = iota((SLOTS, LANES), 0)

    def step(q, _):
        first = pl.multiple_of(q * LANES, LANES)
        here = rows == slots[pl.ds(q, 1), :] % SLOTS
        for v in range(9):
            value = grad[pl.ds(v * 32 + q, 1), :]
            high, low = split2(jnp.where(here, value, 0.0))
            spread[v * 32 : v * 32 + 32, pl.ds(first, LANES)] = high
            spread[288 + v * 32 : 320 + v * 32, pl.ds(first, LANES)] = low
        return 0

    lax.fori_loop(0, STEPS, step, 0, unroll=2)
    for g, size in ((0, 128), (1, 128), (2, 32)):
        high = dot_nt(hot[...], spread[g * 128 : g * 128 + size, :])
        low = dot_nt(hot[...], spread[288 + g * 128 : 288 + g * 128 + size, :])
        msg[:, 0, g * 128 : g * 128 + size] = high + low


def place_of(device):
    return (device // N_PIX, lax.rem(device, N_PIX))


def greet(me):
    barrier = pltpu.get_barrier_semaphore()

    def one(k, _):
        pl.semaphore_signal(barrier, inc=1, device_id=place_of(lax.rem(me + k, N_DEV)), device_id_type=MESH)
        return 0

    lax.fori_loop(1, N_DEV, one, 0)


def await_greetings():
    pl.semaphore_wait(pltpu.get_barrier_semaphore(), N_DEV - 1)


def send_all(me, msg, got, send_sem, recv_sem):
    def one(k, _):
        there = lax.rem(me + k, N_DEV)
        pltpu.make_async_remote_copy(
            src_ref=msg.at[there],
            dst_ref=got.at[me],
            send_sem=send_sem,
            recv_sem=recv_sem,
            device_id=place_of(there),
            device_id_type=MESH,
        ).start()
        return 0

    lax.fori_loop(1, N_DEV, one, 0)
    got[me] = msg[me]


def all_of(me, msg, got, send_sem, recv_sem):
    return pltpu.make_async_remote_copy(
        src_ref=msg.at[pl.ds(0, N_DEV - 1)],
        dst_ref=got.at[pl.ds(0, N_DEV - 1)],
        send_sem=send_sem,
        recv_sem=recv_sem,
        device_id=place_of(lax.rem(me + 1, N_DEV)),
        device_id_type=MESH,
    )


def main_kernel(
    params, lists_next, lists_cur, angles_next, angles_cur, counts_next, counts_cur,
    sends_next, sends_cur, cot, power, moments,
    image, returned, basis_cur,
    ask, asked, msg_cur, got_cur, msg_next, got_next, back, got_back,
    slots_next, slots_cur, hot_next, hot_cur, turned, mark,
    held_params, table, rows, rows_cur, rows_next, row_v, half_next, half_cur, row_next, row_cur, basis_next, color,
    split, entry, factor, alpha, shade, weights, pull, held, cots, sums, grad, spread,
    send_sems, recv_sems, param_sems, index_sems,
):
    me = lax.axis_index("gauss") * N_PIX + lax.axis_index("pix")
    greet(me)
    copies = param_copies(params, held_params, param_sems)
    for copy in copies:
        copy.start()
    split_index(sends_cur, row_v.at[0], half_cur)
    split_index(sends_next, row_v.at[1], half_next)
    to_smem = [
        pltpu.make_async_copy(row_v.at[0], row_cur, index_sems.at[0]),
        pltpu.make_async_copy(row_v.at[1], row_next, index_sems.at[1]),
    ]
    for copy in to_smem:
        copy.start()
    order_lists(lists_next, turned, slots_next)
    owner_onehot(slots_next, hot_next)
    tiles_next = slot_tiles(slots_next, hot_next, mark)
    order_lists(lists_cur, turned, slots_cur)
    owner_onehot(slots_cur, hot_cur)
    tiles_cur = slot_tiles(slots_cur, hot_cur, mark)
    ask[:, 0, :] = angle_message(tiles_next, tiles_cur, angles_next, angles_cur)
    await_greetings()
    links = [
        (me, src, dst, send_sems.at[k], recv_sems.at[k])
        for k, (src, dst) in enumerate(((ask, asked), (msg_cur, got_cur), (msg_next, got_next), (back, got_back)))
    ]
    send_all(*links[0])
    for copy in to_smem:
        copy.wait()
    build_table(copies, held_params, table)
    gather_rows(row_cur, table, rows, half_cur, rows_cur)
    all_of(*links[0]).wait_recv()
    seen = asked[:, 0, :].T
    for k, term in enumerate(sh_terms(seen[64:96], seen[96:128])):
        basis_cur[k * 32 : k * 32 + 32, :] = term
    color_rows(basis_cur, rows_cur, color)
    owner_message(rows_cur, color, msg_cur)
    basis_cur[512:544, :] = jnp.zeros((32, LANES), F32)
    send_all(*links[1])
    for k, term in enumerate(sh_terms(seen[0:32], seen[32:64])):
        basis_next[k * 32 : k * 32 + 32, :] = term
    gather_rows(row_next, table, rows, half_next, rows_next)
    color_rows(basis_next, rows_next, color)
    owner_message(rows_next, color, msg_next)
    send_all(*links[2])
    all_of(*links[1]).wait_recv()
    entries_in_order(got_cur, hot_cur, slots_cur, split, entry)
    power_factors(entry, counts_cur, factor)
    alphas_and_colors(factor, power, alpha, shade)
    weights_forward(alpha, weights)
    backward(alpha, shade, weights, cot, pull, held)
    pixel_sums(pull, held, moments, cot, cots, sums)
    entry_gradients(entry, sums, grad)
    slots_in_order(grad, hot_cur, slots_cur, spread, back)
    back[:, 0, 288:384] = jnp.zeros((N_DEV, 96), F32)
    send_all(*links[3])
    all_of(*links[2]).wait_recv()
    entries_in_order(got_next, hot_next, slots_next, split, entry)
    power_factors(entry, counts_next, factor)
    alphas_and_colors(factor, power, alpha, shade)
    composite(alpha, shade, image)
    all_of(*links[3]).wait_recv()
    for g in range(3):
        returned[g * 128 : g * 128 + 128, :] = got_back[:, 0, g * 128 : g * 128 + 128].T
    for link in links:
        all_of(*link).wait_send()


def scatter_kernel(turned, basis, sends, grads, row_v, half, row_s, total, piece, rows, sem):
    split_index(sends, row_v, half)
    copy = pltpu.make_async_copy(row_v, row_s, sem)
    copy.start()

    def clear(b, _):
        total[pl.ds(pl.multiple_of(b * 256, 256), 256), :] = jnp.zeros((256, LANES), F32)
        return 0

    lax.fori_loop(0, HALF // 256, clear, 0)
    piece[48:64, :] = jnp.zeros((16, LANES), F32)
    same_group = iota((LANES, LANES), 0) // 16 == iota((LANES, LANES), 1) // 16
    copy.wait()

    def slot(r, _):
        piece[0:6, :] = turned[pl.ds(r, 8, stride=32), :][0:6]
        terms = basis[pl.ds(r, 16, stride=32), :]
        for ch in range(3):
            piece[6 + 16 * ch : 22 + 16 * ch, :] = terms * turned[pl.ds((6 + ch) * 32 + r, 1), :]
        upper = half[pl.ds(r, 1), :] > 0
        values = piece[...]
        both = jnp.concatenate([jnp.where(upper, 0.0, values), jnp.where(upper, values, 0.0)], 0)
        high, low = split2(both)
        name = jnp.broadcast_to(row_v[pl.ds(r, 1), :].astype(F32), (LANES, LANES))
        same = jnp.logical_and(name == name.T, same_group).astype(F32).astype(BF16)
        rows[...] = dot_nt(jnp.concatenate([same, same], 1), jnp.concatenate([high, low], 1))
        for g in range(8):
            places = [row_s[r, g * 16 + u] for u in range(16)]
            olds = [total[pl.ds(places[u], 1), :] for u in range(16)]
            for u in range(16):
                total[pl.ds(places[u], 1), :] = olds[u] + rows[g * 16 + u : g * 16 + u + 1, :]
        return 0

    lax.fori_loop(0, SLOTS, slot, 0)

    def block(b, _):
        first = pl.multiple_of(b * LANES, LANES)
        both = total[pl.ds(first, LANES), :].T
        grads[:, pl.ds(first, LANES)] = both[0:ROWS]
        grads[:, pl.ds(first + HALF, LANES)] = both[64 : 64 + ROWS]
        return 0

    lax.fori_loop(0, HALF // LANES, block, 0, unroll=4)


VM = pl.BlockSpec(memory_space=pltpu.VMEM)
SM = pl.BlockSpec(memory_space=pltpu.SMEM)
PARAMS = pltpu.CompilerParams(vmem_limit_bytes=VMEM_LIMIT)


def shape(dims, dtype=F32):
    return jax.ShapeDtypeStruct(dims, dtype)


def body(params, angles_next, angles_cur, lists_next, lists_cur, counts_next, counts_cur, sends_next, sends_cur, cotangent):
    power, moments = pixel_tables()
    dense = (STEPS, LANES)
    wide = pltpu.VMEM((N_DEV, 1, 384), F32)
    image, returned, basis = pl.pallas_call(
        main_kernel,
        out_shape=(shape((3, 16, 256)), shape((384, LANES)), shape((544, LANES))),
        in_specs=[pl.BlockSpec(memory_space=pl.ANY), VM, VM, SM, SM, SM, SM, VM, VM, VM, VM, VM],
        out_specs=(VM,) * 3,
        scratch_shapes=[
            pltpu.VMEM((N_DEV, 1, 128), F32),
            pltpu.VMEM((N_DEV, 1, 128), F32),
            wide, wide, wide, wide, wide, wide,
            pltpu.VMEM(dense, I32),
            pltpu.VMEM(dense, I32),
            pltpu.VMEM((N_DEV, 4096), BF16),
            pltpu.VMEM((N_DEV, 4096), BF16),
            pltpu.VMEM((264, LANES), I32),
            pltpu.VMEM((SLOTS, 4096), BF16),
            pltpu.VMEM((ROWS, GAUSS), F32),
            pltpu.VMEM((HALF, LANES), F32),
            pltpu.VMEM((256, LANES), F32),
            pltpu.VMEM((SLOTS * 64 + 8, LANES), F32),
            pltpu.VMEM((SLOTS * 64 + 8, LANES), F32),
            pltpu.VMEM((2,) + dense, I32),
            pltpu.VMEM(dense, I32),
            pltpu.VMEM(dense, I32),
            pltpu.SMEM(dense, I32),
            pltpu.SMEM(dense, I32),
            pltpu.VMEM((544, LANES), F32),
            pltpu.VMEM((96, LANES), F32),
            pltpu.VMEM((288, 384), BF16),
            pltpu.VMEM((288, LANES), F32),
            pltpu.VMEM((1056, LANES), F32),
            pltpu.VMEM((4096, 256), F32),
            pltpu.VMEM((4096, 384), F32),
            pltpu.VMEM((4096, 256), F32),
            pltpu.VMEM((4096, 512), BF16),
            pltpu.VMEM((4096, 512), BF16),
            pltpu.VMEM((48, 768), BF16),
            pltpu.VMEM((288, LANES), F32),
            pltpu.VMEM((288, LANES), F32),
            pltpu.VMEM((576, 4096), BF16),
            pltpu.SemaphoreType.DMA((4,)),
            pltpu.SemaphoreType.DMA((4,)),
            pltpu.SemaphoreType.DMA((2 * CHUNKS,)),
            pltpu.SemaphoreType.DMA((2,)),
        ],
        compiler_params=pltpu.CompilerParams(
            vmem_limit_bytes=VMEM_LIMIT, collective_id=0, has_side_effects=True
        ),
        name="main",
    )(params, lists_next, lists_cur, angles_next, angles_cur, counts_next, counts_cur,
      sends_next[0], sends_cur[0], jnp.transpose(cotangent, (1, 0, 2)), power, moments)
    grads = pl.pallas_call(
        scatter_kernel,
        out_shape=shape((ROWS, GAUSS)),
        in_specs=[VM] * 3,
        out_specs=VM,
        scratch_shapes=[
            pltpu.VMEM(dense, I32),
            pltpu.VMEM(dense, I32),
            pltpu.SMEM(dense, I32),
            pltpu.VMEM((HALF, LANES), F32),
            pltpu.VMEM((64, LANES), F32),
            pltpu.VMEM((LANES, LANES), F32),
            pltpu.SemaphoreType.DMA,
        ],
        compiler_params=PARAMS,
        name="scatter",
    )(returned, basis, sends_cur[0])
    return jnp.transpose(image, (1, 0, 2)), grads


def solution(mesh):
    both = ("gauss", "pix")
    placed = (
        P(None, both),
        P(both, None),
        P(both, None),
        P(both, None),
        P(both, None),
        P(both),
        P(both),
        P(both, None, None),
        P(both, None, None),
        P(both, None, None),
    )
    return jax.shard_map(
        body,
        mesh=mesh,
        in_specs=placed,
        out_specs=(P(both, None, None), P(None, both)),
        check_vma=False,
    )
```

```python
import jax
import jax.numpy as jnp
import numpy as np
from jax import lax
from jax.experimental import pallas as pl
from jax.experimental.pallas import tpu as pltpu
from jax.sharding import PartitionSpec as P

F32 = jnp.float32
BF16 = jnp.bfloat16
I32 = jnp.int32
MESH = pl.DeviceIdType.MESH
N_DEV = 128
N_PIX = 32
SLOTS = 32
GAUSS = 16384
HALF = 8192
CHUNKS = 4
UNROLL_ENTRY = 8
UNROLL_ALPHA = 8
GROUP = 8
ROWS = 54
LANES = 128
STEPS = 32
LOG2E = 1.4426950408889634
VMEM_LIMIT = 56 * 2**20


def iota(shape, dim):
    return lax.broadcasted_iota(I32, shape, dim)


def dot_nn(a, b):
    return lax.dot_general(a, b, (((1,), (0,)), ((), ())), preferred_element_type=F32)


def dot_nt(a, b):
    return lax.dot_general(a, b, (((1,), (1,)), ((), ())), preferred_element_type=F32)


def split2(x):
    high = x.astype(BF16)
    low = (x - high.astype(F32)).astype(BF16)
    return high, low


def split3(x):
    high = x.astype(BF16)
    rest = x - high.astype(F32)
    mid = rest.astype(BF16)
    low = (rest - mid.astype(F32)).astype(BF16)
    return high, mid, low


def pixel_tables():
    pixels = np.arange(256)
    qx = (pixels % 16) - 7.5
    qy = (pixels // 16) - 7.5
    mono = np.stack([np.ones(256), qx, qy, qx * qx, qx * qy, qy * qy], 0)
    power = np.zeros((32, 640), np.float32)
    for part in range(3):
        power[part * 6 : part * 6 + 6, :256] = mono
        for ch in range(3):
            power[18 + part * 3 + ch, 256 + 128 * ch : 384 + 128 * ch] = 1.0
    moments = np.zeros((16, 512), np.float32)
    moments[:6, :256] = mono
    moments[:6, 256:] = mono
    return jnp.asarray(power, BF16), jnp.asarray(moments, BF16)


def order_lists(lists_ref, turned, slots_ref):
    turned[0:256, 0:16] = lists_ref[...].T
    lane_group = iota((STEPS, LANES), 1) // 16
    out = jnp.zeros((STEPS, LANES), I32)
    for k in range(8):
        piece = pltpu.roll(turned[pl.ds(k, STEPS, stride=8), :], 16 * k, 1) if k else turned[pl.ds(0, STEPS, stride=8), :]
        out = jnp.where(lane_group == k, piece, out)
    slots_ref[...] = out


def owner_onehot(slots_ref, hot_ref):
    rows = iota((N_DEV, LANES), 0)
    for q in range(STEPS):
        owner = slots_ref[q : q + 1, :] // SLOTS
        hot_ref[:, q * LANES : (q + 1) * LANES] = (rows == owner).astype(F32).astype(BF16)


def slot_tiles(slots_ref, hot_ref, mark_ref):
    rows = iota((SLOTS, LANES), 0)
    tile = (iota((SLOTS, LANES), 1) % 16).astype(F32)
    for q in range(STEPS):
        place = slots_ref[q : q + 1, :] % SLOTS
        mark_ref[:, q * LANES : (q + 1) * LANES] = jnp.where(rows == place, tile, 0.0).astype(BF16)
    return dot_nt(hot_ref[...], mark_ref[...])


def angle_message(tiles_next, tiles_cur, angles_next, angles_cur):
    tiles = jnp.concatenate([tiles_next, tiles_next, tiles_cur, tiles_cur], 1)
    region = iota((1, LANES), 1) // 32
    out = jnp.zeros((N_DEV, LANES), F32)
    for t in range(16):
        row = jnp.where(
            region < 2,
            jnp.where(region == 0, angles_next[0, t], angles_next[1, t]),
            jnp.where(region == 2, angles_cur[0, t], angles_cur[1, t]),
        )
        out = jnp.where(tiles == float(t), row, out)
    return out


def sh_terms(theta, azimuth):
    sin_t = jnp.sin(theta)
    dir_x = sin_t * jnp.cos(azimuth)
    dir_y = sin_t * jnp.sin(azimuth)
    dir_z = jnp.cos(theta)
    sq_x = dir_x * dir_x
    sq_y = dir_y * dir_y
    sq_z = dir_z * dir_z
    return [
        0.28209479177387814 * jnp.ones_like(dir_x),
        -0.4886025119029199 * dir_y,
        0.4886025119029199 * dir_z,
        -0.4886025119029199 * dir_x,
        1.0925484305920792 * dir_x * dir_y,
        -1.0925484305920792 * dir_y * dir_z,
        0.31539156525252005 * (2.0 * sq_z - sq_x - sq_y),
        -1.0925484305920792 * dir_x * dir_z,
        0.5462742152960396 * (sq_x - sq_y),
        -0.5900435899266435 * dir_y * (3.0 * sq_x - sq_y),
        2.890611442640554 * dir_x * dir_y * dir_z,
        -0.4570457994644658 * dir_y * (4.0 * sq_z - sq_x - sq_y),
        0.3731763325901154 * dir_z * (2.0 * sq_z - 3.0 * sq_x - 3.0 * sq_y),
        -0.4570457994644658 * dir_x * (4.0 * sq_z - sq_x - sq_y),
        1.445305721320277 * dir_z * (sq_x - sq_y),
        -0.5900435899266435 * dir_x * (sq_x - 3.0 * sq_y),
    ]


def param_copies(params, held, sems):
    width = HALF // CHUNKS
    out = []
    for c in range(CHUNKS):
        for k in range(2):
            cols = pl.ds(k * HALF + c * width, width)
            out.append(pltpu.make_async_copy(params.at[:, cols], held.at[:, cols], sems.at[c * 2 + k]))
    return out


def build_table(copies, params, table):
    zeros = jnp.zeros((64 - ROWS, LANES), F32)
    blocks = HALF // LANES // CHUNKS

    for c in range(CHUNKS):
        copies[c * 2].wait()
        copies[c * 2 + 1].wait()

        def block(b, _):
            first = pl.multiple_of((c * blocks + b) * LANES, LANES)
            both = jnp.concatenate(
                [params[:, pl.ds(first, LANES)], zeros, params[:, pl.ds(first + HALF, LANES)], zeros], 0
            )
            table[pl.ds(first, LANES), :] = both.T
            return 0

        lax.fori_loop(0, blocks, block, 0, unroll=8)


def gather_rows(index, table, rows, half_ref, turned):
    def some(step, _):
        for k in range(GROUP):
            for d in range(LANES):
                place = index[step * GROUP + k, d]
                rows[k * 128 + d : k * 128 + d + 1, :] = table[pl.ds(place, 1), :]
        for k in range(GROUP):
            r = step * GROUP + k
            both = rows[k * 128 : k * 128 + 128, :].T
            upper = half_ref[pl.ds(r, 1), :] > 0
            turned[pl.ds(pl.multiple_of(r * 64, 64), 64), :] = jnp.where(upper, both[64:], both[:64])
        return 0

    lax.fori_loop(0, SLOTS // GROUP, some, 0)


def split_index(sends_ref, row_ref, half_ref):
    turned = sends_ref[...]
    half_ref[...] = turned // HALF
    row_ref[...] = turned % HALF


def color_rows(basis, turned, color):
    def one(r, _):
        terms = basis[pl.ds(r, 16, stride=32), :]
        for ch in range(3):
            start = r * 64 + 6 + 16 * ch
            color[pl.ds(ch * 32 + r, 1), :] = 0.5 + jnp.sum(terms * turned[pl.ds(start, 16), :], axis=0, keepdims=True)
        return 0

    lax.fori_loop(0, SLOTS, one, 0, unroll=4)


def owner_message(turned, color, msg):
    geo = [turned[pl.ds(v, 32, stride=64), :] for v in range(6)]
    msg[:, 0, 0:128] = jnp.concatenate(geo[0:4], 0).T
    msg[:, 0, 128:256] = jnp.concatenate([geo[4], geo[5], color[0:32], color[32:64]], 0).T
    last = color[64:96]
    msg[:, 0, 256:384] = jnp.concatenate([last, last, last, last], 0).T


def entries_in_order(got, hot, slots, split, entry):
    zero = jnp.zeros((32, LANES), BF16)
    fine = {0: 288, 1: 320, 5: 352}
    for g, size in ((0, 128), (1, 128), (2, 32)):
        high, mid, low = split3(got[:, 0, g * 128 : g * 128 + 128].T[0:size])
        split[g * 128 : g * 128 + size, 0:128] = high
        split[g * 128 : g * 128 + size, 128:256] = mid
        for v, row in fine.items():
            if v // 4 == g:
                first = (v - g * 4) * 32
                split[row : row + 32, 0:128] = low[first : first + 32]
                split[row : row + 32, 128:256] = zero
    rows = iota((SLOTS, LANES), 0)

    def step(q, _):
        cols = hot[:, pl.ds(pl.multiple_of(q * LANES, LANES), LANES)]
        picked = dot_nn(split[...], jnp.concatenate([cols, cols], 0))
        here = rows == slots[pl.ds(q, 1), :] % SLOTS
        for v in range(9):
            value = picked[v * 32 : v * 32 + 32]
            if v in fine:
                value = value + picked[fine[v] : fine[v] + 32]
            kept = jnp.where(here, value, 0.0)
            entry[pl.ds(v * 32 + q, 1), :] = jnp.sum(kept, axis=0, keepdims=True)
        return 0

    lax.fori_loop(0, STEPS, step, 0, unroll=UNROLL_ENTRY)


def power_factors(entry, counts, factor):
    x = entry[0:32] - 8.0
    y = entry[32:64] - 8.0
    con_a = entry[64:96]
    con_b = entry[96:128]
    con_c = entry[128:160]
    logit = entry[160:192]
    position = iota((STEPS, LANES), 0) * 8 + iota((STEPS, LANES), 1) // 16
    tile = iota((STEPS, LANES), 1) % 16
    count = jnp.zeros((STEPS, LANES), I32)
    for t in range(16):
        count = jnp.where(tile == t, counts[t], count)
    live = position < count
    lin_x = con_a * x + con_b * y
    lin_y = con_b * x + con_c * y
    const = -0.5 * (x * lin_x + y * lin_y) - jnp.log(1.0 + jnp.exp(-logit))
    factors = [const, lin_x, lin_y, -0.5 * con_a, -con_b, -0.5 * con_c]
    for k, value in enumerate(factors):
        value = jnp.where(live, value * LOG2E, -1000.0 if k == 0 else 0.0)
        for p, part in enumerate(split3(value)):
            row = (p * 6 + k) * 32
            factor[row : row + 32, :] = part.astype(F32)
    for ch in range(3):
        for p, part in enumerate(split3(entry[192 + ch * 32 : 224 + ch * 32])):
            row = (18 + p * 3 + ch) * 32
            factor[row : row + 32, :] = part.astype(F32)
    factor[27 * 32 : 32 * 32, :] = jnp.zeros((5 * 32, LANES), F32)


def alphas_and_colors(factor, power, alpha, shade):
    def step(q, _):
        first = pl.multiple_of(q * LANES, LANES)
        left = factor[pl.ds(q, 32, stride=32), :].T.astype(BF16)
        out = dot_nn(left, power[...])
        alpha[pl.ds(first, LANES), :] = jnp.minimum(jnp.exp2(out[:, 0:256]), 0.99)
        shade[pl.ds(first, LANES), :] = out[:, 256:640]
        return 0

    lax.fori_loop(0, STEPS, step, 0, unroll=UNROLL_ALPHA)


def composite(alpha, shade, image):
    one = jnp.ones((16, LANES), F32)
    zero = jnp.zeros((16, LANES), F32)

    def step(q, state):
        through = list(state[0:2])
        total = list(state[2:8])
        for k in range(8):
            row = pl.ds(pl.multiple_of(q * LANES + k * 16, 16), 16)
            colors = [shade[row, ch * 128 : ch * 128 + 128] for ch in range(3)]
            for h in range(2):
                weight = alpha[row, h * 128 : h * 128 + 128] * through[h]
                through[h] = through[h] - weight
                for ch in range(3):
                    total[ch * 2 + h] = total[ch * 2 + h] + weight * colors[ch]
        return tuple(through + total)

    state = lax.fori_loop(0, STEPS, step, (one, one) + (zero,) * 6)
    for ch in range(3):
        for h in range(2):
            image[ch, :, h * 128 : h * 128 + 128] = state[2 + ch * 2 + h]


def weights_forward(alpha, weights):
    one = jnp.ones((16, LANES), F32)

    def step(q, through):
        through = list(through)
        for k in range(8):
            row = pl.ds(pl.multiple_of(q * LANES + k * 16, 16), 16)
            for h in range(2):
                weight = alpha[row, h * 128 : h * 128 + 128] * through[h]
                through[h] = through[h] - weight
                weights[row, h * 128 : h * 128 + 128] = weight
        return tuple(through)

    lax.fori_loop(0, STEPS, step, (one, one))


def backward(alpha, shade, weights, cot, parts):
    up = [cot[ch, :, h * 128 : h * 128 + 128] for ch in range(3) for h in range(2)]
    zero = jnp.zeros((16, LANES), F32)

    def step(s, behind):
        behind = list(behind)
        q = STEPS - 1 - s
        for k in range(7, -1, -1):
            row = pl.ds(pl.multiple_of(q * LANES + k * 16, 16), 16)
            colors = [shade[row, ch * 128 : ch * 128 + 128] for ch in range(3)]
            for h in range(2):
                opaque = alpha[row, h * 128 : h * 128 + 128]
                weight = weights[row, h * 128 : h * 128 + 128]
                value = up[h] * colors[0] + up[2 + h] * colors[1] + up[4 + h] * colors[2]
                ahead = value - behind[h]
                behind[h] = behind[h] + opaque * ahead
                pulled = jnp.where(opaque < 0.99, weight * ahead, 0.0)
                pieces = split2(pulled) + split2(weight)
                for p, piece in enumerate(pieces):
                    parts[row, p * 256 + h * 128 : p * 256 + h * 128 + 128] = piece
        return tuple(behind)

    lax.fori_loop(0, STEPS, step, (zero, zero))


def pixel_sums(parts, moments, cot, against, sums):
    high, low = split2(cot[...].reshape(48, 256))
    against[...] = jnp.zeros((LANES, 1024), BF16)
    against[0:16, 0:512] = moments[...]
    against[16:64, 512:768] = high
    against[16:64, 768:1024] = high
    against[64:112, 512:768] = low
    own = iota((16, LANES), 0) == iota((16, LANES), 1) % 16

    def step(s, _):
        row = pl.ds(pl.multiple_of(s * 1024, 1024), 1024)
        totals = dot_nt(parts[row, :], against[...])
        for k in range(8):
            q = s * 8 + k
            turned = totals[k * 128 : k * 128 + 128].T
            for v in range(6):
                sums[pl.ds(v * 32 + q, 1), :] = turned[v : v + 1]
            for ch in range(3):
                first = 16 + ch * 16
                value = turned[first : first + 16] + turned[first + 48 : first + 64]
                kept = jnp.where(own, value, 0.0)
                sums[pl.ds((6 + ch) * 32 + q, 1), :] = jnp.sum(kept, axis=0, keepdims=True)
        return 0

    lax.fori_loop(0, STEPS // 8, step, 0)


def entry_gradients(entry, sums, grad):
    x = entry[0:32] - 8.0
    y = entry[32:64] - 8.0
    con_a = entry[64:96]
    con_b = entry[96:128]
    con_c = entry[128:160]
    fade = jnp.exp(-entry[160:192])
    s_0 = sums[0:32]
    s_x = sums[32:64]
    s_y = sums[64:96]
    d_x = s_x - x * s_0
    d_y = s_y - y * s_0
    d_xx = sums[96:128] - x * (s_x + d_x)
    d_xy = sums[128:160] - x * s_y - y * d_x
    d_yy = sums[160:192] - y * (s_y + d_y)
    values = [
        con_a * d_x + con_b * d_y,
        con_b * d_x + con_c * d_y,
        -0.5 * d_xx,
        -d_xy,
        -0.5 * d_yy,
        s_0 * (fade / (1.0 + fade)),
        sums[192:224],
        sums[224:256],
        sums[256:288],
    ]
    for v, value in enumerate(values):
        grad[v * 32 : v * 32 + 32, :] = value


def slots_in_order(grad, hot, slots, spread, msg):
    rows = iota((SLOTS, LANES), 0)

    def step(q, _):
        first = pl.multiple_of(q * LANES, LANES)
        here = rows == slots[pl.ds(q, 1), :] % SLOTS
        for v in range(9):
            value = grad[pl.ds(v * 32 + q, 1), :]
            high, low = split2(jnp.where(here, value, 0.0))
            spread[v * 32 : v * 32 + 32, pl.ds(first, LANES)] = high
            spread[288 + v * 32 : 320 + v * 32, pl.ds(first, LANES)] = low
        return 0

    lax.fori_loop(0, STEPS, step, 0, unroll=2)
    for g, size in ((0, 128), (1, 128), (2, 32)):
        high = dot_nt(hot[...], spread[g * 128 : g * 128 + size, :])
        low = dot_nt(hot[...], spread[288 + g * 128 : 288 + g * 128 + size, :])
        msg[:, 0, g * 128 : g * 128 + size] = high + low


def place_of(device):
    return (device // N_PIX, lax.rem(device, N_PIX))


def greet(me):
    barrier = pltpu.get_barrier_semaphore()

    def one(k, _):
        pl.semaphore_signal(barrier, inc=1, device_id=place_of(lax.rem(me + k, N_DEV)), device_id_type=MESH)
        return 0

    lax.fori_loop(1, N_DEV, one, 0, unroll=8)


def await_greetings():
    pl.semaphore_wait(pltpu.get_barrier_semaphore(), N_DEV - 1)


def send_all(me, msg, got, send_sem, recv_sem):
    def one(k, _):
        there = lax.rem(me + k, N_DEV)
        pltpu.make_async_remote_copy(
            src_ref=msg.at[there],
            dst_ref=got.at[me],
            send_sem=send_sem,
            recv_sem=recv_sem,
            device_id=place_of(there),
            device_id_type=MESH,
        ).start()
        return 0

    lax.fori_loop(1, N_DEV, one, 0, unroll=8)
    got[me] = msg[me]


def all_of(me, msg, got, send_sem, recv_sem):
    return pltpu.make_async_remote_copy(
        src_ref=msg.at[pl.ds(0, N_DEV - 1)],
        dst_ref=got.at[pl.ds(0, N_DEV - 1)],
        send_sem=send_sem,
        recv_sem=recv_sem,
        device_id=place_of(lax.rem(me + 1, N_DEV)),
        device_id_type=MESH,
    )


def main_kernel(
    params, lists_next, lists_cur, angles_next, angles_cur, counts_next, counts_cur,
    sends_next, sends_cur, cot, power, moments,
    image, returned, basis_cur,
    ask, asked, msg_cur, got_cur, msg_next, got_next, back, got_back,
    slots_next, slots_cur, hot_next, hot_cur, turned, mark,
    held_params, table, rows, rows_cur, rows_next, row_v, half_next, half_cur, row_next, row_cur, basis_next, color,
    split, entry, factor, alpha, shade, weights, parts, against, sums, grad, spread,
    send_sems, recv_sems, param_sems, index_sems,
):
    me = lax.axis_index("gauss") * N_PIX + lax.axis_index("pix")
    greet(me)
    copies = param_copies(params, held_params, param_sems)
    for copy in copies:
        copy.start()
    split_index(sends_cur, row_v.at[0], half_cur)
    split_index(sends_next, row_v.at[1], half_next)
    to_smem = [
        pltpu.make_async_copy(row_v.at[0], row_cur, index_sems.at[0]),
        pltpu.make_async_copy(row_v.at[1], row_next, index_sems.at[1]),
    ]
    for copy in to_smem:
        copy.start()
    order_lists(lists_next, turned, slots_next)
    owner_onehot(slots_next, hot_next)
    tiles_next = slot_tiles(slots_next, hot_next, mark)
    order_lists(lists_cur, turned, slots_cur)
    owner_onehot(slots_cur, hot_cur)
    tiles_cur = slot_tiles(slots_cur, hot_cur, mark)
    ask[:, 0, :] = angle_message(tiles_next, tiles_cur, angles_next, angles_cur)
    for copy in to_smem:
        copy.wait()
    build_table(copies, held_params, table)
    await_greetings()
    links = [
        (me, src, dst, send_sems.at[k], recv_sems.at[k])
        for k, (src, dst) in enumerate(((ask, asked), (msg_cur, got_cur), (msg_next, got_next), (back, got_back)))
    ]
    send_all(*links[0])
    gather_rows(row_cur, table, rows, half_cur, rows_cur)
    all_of(*links[0]).wait_recv()
    seen = asked[:, 0, :].T
    for k, term in enumerate(sh_terms(seen[64:96], seen[96:128])):
        basis_cur[k * 32 : k * 32 + 32, :] = term
    color_rows(basis_cur, rows_cur, color)
    owner_message(rows_cur, color, msg_cur)
    basis_cur[512:544, :] = jnp.zeros((32, LANES), F32)
    send_all(*links[1])
    for k, term in enumerate(sh_terms(seen[0:32], seen[32:64])):
        basis_next[k * 32 : k * 32 + 32, :] = term
    gather_rows(row_next, table, rows, half_next, rows_next)
    color_rows(basis_next, rows_next, color)
    owner_message(rows_next, color, msg_next)
    send_all(*links[2])
    all_of(*links[1]).wait_recv()
    entries_in_order(got_cur, hot_cur, slots_cur, split, entry)
    power_factors(entry, counts_cur, factor)
    alphas_and_colors(factor, power, alpha, shade)
    weights_forward(alpha, weights)
    backward(alpha, shade, weights, cot, parts)
    pixel_sums(parts, moments, cot, against, sums)
    entry_gradients(entry, sums, grad)
    slots_in_order(grad, hot_cur, slots_cur, spread, back)
    back[:, 0, 288:384] = jnp.zeros((N_DEV, 96), F32)
    send_all(*links[3])
    all_of(*links[2]).wait_recv()
    entries_in_order(got_next, hot_next, slots_next, split, entry)
    power_factors(entry, counts_next, factor)
    alphas_and_colors(factor, power, alpha, shade)
    composite(alpha, shade, image)
    all_of(*links[3]).wait_recv()
    for g in range(3):
        returned[g * 128 : g * 128 + 128, :] = got_back[:, 0, g * 128 : g * 128 + 128].T
    for link in links:
        all_of(*link).wait_send()


def scatter_kernel(turned, basis, sends, grads, row_v, half, row_s, total, piece, rows, out, sem, out_sems):
    split_index(sends, row_v, half)
    copy = pltpu.make_async_copy(row_v, row_s, sem)
    copy.start()

    def clear(b, _):
        total[pl.ds(pl.multiple_of(b * 512, 512), 512), :] = jnp.zeros((512, LANES), F32)
        return 0

    piece[...] = jnp.zeros((2, 64, LANES), F32)
    same_group = iota((LANES, LANES), 0) // 16 == iota((LANES, LANES), 1) // 16

    def prepare(r, k):
        piece[k, 0:6, :] = turned[pl.ds(r, 8, stride=32), :][0:6]
        terms = basis[pl.ds(r, 16, stride=32), :]
        for ch in range(3):
            piece[k, 6 + 16 * ch : 22 + 16 * ch, :] = terms * turned[pl.ds((6 + ch) * 32 + r, 1), :]
        upper = half[pl.ds(r, 1), :] > 0
        values = piece[k]
        both = jnp.concatenate([jnp.where(upper, 0.0, values), jnp.where(upper, values, 0.0)], 0)
        high, low = split2(both)
        name = jnp.broadcast_to(row_v[pl.ds(r, 1), :].astype(F32), (LANES, LANES))
        same = jnp.logical_and(name == name.T, same_group).astype(F32).astype(BF16)
        rows[k] = dot_nt(jnp.concatenate([same, same], 1), jnp.concatenate([high, low], 1))

    def add(r, k):
        for g in range(8):
            places = [row_s[r, g * 16 + u] for u in range(16)]
            olds = [total[pl.ds(places[u], 1), :] for u in range(16)]
            for u in range(16):
                total[pl.ds(places[u], 1), :] = olds[u] + rows[k, g * 16 + u : g * 16 + u + 1, :]

    prepare(0, 0)
    lax.fori_loop(0, HALF // 512, clear, 0)
    copy.wait()

    def slots(s, _):
        prepare(s * 2 + 1, 1)
        add(s * 2, 0)
        prepare(lax.rem(s * 2 + 2, SLOTS), 0)
        add(s * 2 + 1, 1)
        return 0

    lax.fori_loop(0, SLOTS // 2, slots, 0)

    width = HALF // CHUNKS
    writes = []
    for c in range(CHUNKS):
        def block(b, _):
            first = pl.multiple_of(c * width + b * LANES, LANES)
            both = total[pl.ds(first, LANES), :].T
            out[:, pl.ds(first, LANES)] = both[0:ROWS]
            out[:, pl.ds(first + HALF, LANES)] = both[64 : 64 + ROWS]
            return 0

        lax.fori_loop(0, width // LANES, block, 0, unroll=8)
        for k in range(2):
            cols = pl.ds(k * HALF + c * width, width)
            write = pltpu.make_async_copy(out.at[:, cols], grads.at[:, cols], out_sems.at[c * 2 + k])
            write.start()
            writes.append(write)
    for write in writes:
        write.wait()


VM = pl.BlockSpec(memory_space=pltpu.VMEM)
SM = pl.BlockSpec(memory_space=pltpu.SMEM)
PARAMS = pltpu.CompilerParams(vmem_limit_bytes=VMEM_LIMIT)


def shape(dims, dtype=F32):
    return jax.ShapeDtypeStruct(dims, dtype)


def body(params, angles_next, angles_cur, lists_next, lists_cur, counts_next, counts_cur, sends_next, sends_cur, cotangent):
    power, moments = pixel_tables()
    dense = (STEPS, LANES)
    wide = pltpu.VMEM((N_DEV, 1, 384), F32)
    image, returned, basis = pl.pallas_call(
        main_kernel,
        out_shape=(shape((3, 16, 256)), shape((384, LANES)), shape((544, LANES))),
        in_specs=[pl.BlockSpec(memory_space=pl.ANY), VM, VM, SM, SM, SM, SM, VM, VM, VM, VM, VM],
        out_specs=(VM,) * 3,
        scratch_shapes=[
            pltpu.VMEM((N_DEV, 1, 128), F32),
            pltpu.VMEM((N_DEV, 1, 128), F32),
            wide, wide, wide, wide, wide, wide,
            pltpu.VMEM(dense, I32),
            pltpu.VMEM(dense, I32),
            pltpu.VMEM((N_DEV, 4096), BF16),
            pltpu.VMEM((N_DEV, 4096), BF16),
            pltpu.VMEM((264, LANES), I32),
            pltpu.VMEM((SLOTS, 4096), BF16),
            pltpu.VMEM((ROWS, GAUSS), F32),
            pltpu.VMEM((HALF, LANES), F32),
            pltpu.VMEM((GROUP * LANES, LANES), F32),
            pltpu.VMEM((SLOTS * 64 + 8, LANES), F32),
            pltpu.VMEM((SLOTS * 64 + 8, LANES), F32),
            pltpu.VMEM((2,) + dense, I32),
            pltpu.VMEM(dense, I32),
            pltpu.VMEM(dense, I32),
            pltpu.SMEM(dense, I32),
            pltpu.SMEM(dense, I32),
            pltpu.VMEM((544, LANES), F32),
            pltpu.VMEM((96, LANES), F32),
            pltpu.VMEM((384, 256), BF16),
            pltpu.VMEM((288, LANES), F32),
            pltpu.VMEM((1056, LANES), F32),
            pltpu.VMEM((4096, 256), F32),
            pltpu.VMEM((4096, 384), F32),
            pltpu.VMEM((4096, 256), F32),
            pltpu.VMEM((4096, 1024), BF16),
            pltpu.VMEM((LANES, 1024), BF16),
            pltpu.VMEM((288, LANES), F32),
            pltpu.VMEM((288, LANES), F32),
            pltpu.VMEM((576, 4096), BF16),
            pltpu.SemaphoreType.DMA((4,)),
            pltpu.SemaphoreType.DMA((4,)),
            pltpu.SemaphoreType.DMA((2 * CHUNKS,)),
            pltpu.SemaphoreType.DMA((2,)),
        ],
        compiler_params=pltpu.CompilerParams(
            vmem_limit_bytes=VMEM_LIMIT, collective_id=0, has_side_effects=True
        ),
        name="main",
    )(params, lists_next, lists_cur, jnp.transpose(angles_next), jnp.transpose(angles_cur), counts_next, counts_cur,
      jnp.transpose(sends_next[0]), jnp.transpose(sends_cur[0]), jnp.transpose(cotangent, (1, 0, 2)), power, moments)
    grads = pl.pallas_call(
        scatter_kernel,
        out_shape=shape((ROWS, GAUSS)),
        in_specs=[VM] * 3,
        out_specs=pl.BlockSpec(memory_space=pl.ANY),
        scratch_shapes=[
            pltpu.VMEM(dense, I32),
            pltpu.VMEM(dense, I32),
            pltpu.SMEM(dense, I32),
            pltpu.VMEM((HALF, LANES), F32),
            pltpu.VMEM((2, 64, LANES), F32),
            pltpu.VMEM((2, LANES, LANES), F32),
            pltpu.VMEM((ROWS, GAUSS), F32),
            pltpu.SemaphoreType.DMA,
            pltpu.SemaphoreType.DMA((2 * CHUNKS,)),
        ],
        compiler_params=PARAMS,
        name="scatter",
    )(returned, basis, jnp.transpose(sends_cur[0]))
    return jnp.transpose(image, (1, 0, 2)), grads


def solution(mesh):
    both = ("gauss", "pix")
    placed = (
        P(None, both),
        P(both, None),
        P(both, None),
        P(both, None),
        P(both, None),
        P(both),
        P(both),
        P(both, None, None),
        P(both, None, None),
        P(both, None, None),
    )
    return jax.shard_map(
        body,
        mesh=mesh,
        in_specs=placed,
        out_specs=(P(both, None, None), P(None, both)),
        check_vma=False,
    )
```

```python
import jax
import jax.numpy as jnp
import numpy as np
from jax import lax
from jax.experimental import pallas as pl
from jax.experimental.pallas import tpu as pltpu
from jax.sharding import PartitionSpec as P

F32 = jnp.float32
BF16 = jnp.bfloat16
I32 = jnp.int32
MESH = pl.DeviceIdType.MESH
N_DEV = 128
N_PIX = 32
SLOTS = 32
GAUSS = 16384
HALF = 8192
CHUNKS = 4
UNROLL_ENTRY = 8
BACK = 4
PAIR = 8
WIDE = 2
UNROLL_ALPHA = 8
GROUP = 8
ROWS = 54
LANES = 128
STEPS = 32
LOG2E = 1.4426950408889634
VMEM_LIMIT = 56 * 2**20


def iota(shape, dim):
    return lax.broadcasted_iota(I32, shape, dim)


def dot_nn(a, b):
    return lax.dot_general(a, b, (((1,), (0,)), ((), ())), preferred_element_type=F32)


def dot_nt(a, b):
    return lax.dot_general(a, b, (((1,), (1,)), ((), ())), preferred_element_type=F32)


def split2(x):
    high = x.astype(BF16)
    low = (x - high.astype(F32)).astype(BF16)
    return high, low


def split3(x):
    high = x.astype(BF16)
    rest = x - high.astype(F32)
    mid = rest.astype(BF16)
    low = (rest - mid.astype(F32)).astype(BF16)
    return high, mid, low


def pixel_tables():
    pixels = np.arange(256)
    qx = (pixels % 16) - 7.5
    qy = (pixels // 16) - 7.5
    mono = np.stack([np.ones(256), qx, qy, qx * qx, qx * qy, qy * qy], 0)
    power = np.zeros((32, 640), np.float32)
    for part in range(3):
        power[part * 6 : part * 6 + 6, :256] = mono
        for ch in range(3):
            power[18 + part * 3 + ch, 256 + 128 * ch : 384 + 128 * ch] = 1.0
    moments = np.zeros((16, 512), np.float32)
    moments[:6, :256] = mono
    moments[:6, 256:] = mono
    return jnp.asarray(power, BF16), jnp.asarray(moments, BF16)


def order_lists(lists_ref, turned, slots_ref):
    turned[0:256, 0:16] = lists_ref[...].T
    lane_group = iota((STEPS, LANES), 1) // 16
    out = jnp.zeros((STEPS, LANES), I32)
    for k in range(8):
        piece = pltpu.roll(turned[pl.ds(k, STEPS, stride=8), :], 16 * k, 1) if k else turned[pl.ds(0, STEPS, stride=8), :]
        out = jnp.where(lane_group == k, piece, out)
    slots_ref[...] = out


def owner_onehot(slots_ref, hot_ref):
    rows = iota((N_DEV, LANES), 0)
    for q in range(STEPS):
        owner = slots_ref[q : q + 1, :] // SLOTS
        hot_ref[:, q * LANES : (q + 1) * LANES] = (rows == owner).astype(F32).astype(BF16)


def slot_tiles(slots_ref, hot_ref, mark_ref):
    rows = iota((SLOTS, LANES), 0)
    tile = (iota((SLOTS, LANES), 1) % 16).astype(F32)
    for q in range(STEPS):
        place = slots_ref[q : q + 1, :] % SLOTS
        mark_ref[:, q * LANES : (q + 1) * LANES] = jnp.where(rows == place, tile, 0.0).astype(BF16)
    return dot_nt(hot_ref[...], mark_ref[...])


def angle_message(tiles_next, tiles_cur, angles_next, angles_cur):
    tiles = jnp.concatenate([tiles_next, tiles_next, tiles_cur, tiles_cur], 1)
    region = iota((1, LANES), 1) // 32
    out = jnp.zeros((N_DEV, LANES), F32)
    for t in range(16):
        row = jnp.where(
            region < 2,
            jnp.where(region == 0, angles_next[0, t], angles_next[1, t]),
            jnp.where(region == 2, angles_cur[0, t], angles_cur[1, t]),
        )
        out = jnp.where(tiles == float(t), row, out)
    return out


def sh_terms(theta, azimuth):
    sin_t = jnp.sin(theta)
    dir_x = sin_t * jnp.cos(azimuth)
    dir_y = sin_t * jnp.sin(azimuth)
    dir_z = jnp.cos(theta)
    sq_x = dir_x * dir_x
    sq_y = dir_y * dir_y
    sq_z = dir_z * dir_z
    return [
        0.28209479177387814 * jnp.ones_like(dir_x),
        -0.4886025119029199 * dir_y,
        0.4886025119029199 * dir_z,
        -0.4886025119029199 * dir_x,
        1.0925484305920792 * dir_x * dir_y,
        -1.0925484305920792 * dir_y * dir_z,
        0.31539156525252005 * (2.0 * sq_z - sq_x - sq_y),
        -1.0925484305920792 * dir_x * dir_z,
        0.5462742152960396 * (sq_x - sq_y),
        -0.5900435899266435 * dir_y * (3.0 * sq_x - sq_y),
        2.890611442640554 * dir_x * dir_y * dir_z,
        -0.4570457994644658 * dir_y * (4.0 * sq_z - sq_x - sq_y),
        0.3731763325901154 * dir_z * (2.0 * sq_z - 3.0 * sq_x - 3.0 * sq_y),
        -0.4570457994644658 * dir_x * (4.0 * sq_z - sq_x - sq_y),
        1.445305721320277 * dir_z * (sq_x - sq_y),
        -0.5900435899266435 * dir_x * (sq_x - 3.0 * sq_y),
    ]


def param_copies(params, held, sems):
    width = HALF // CHUNKS
    out = []
    for c in range(CHUNKS):
        for k in range(2):
            cols = pl.ds(k * HALF + c * width, width)
            out.append(pltpu.make_async_copy(params.at[:, cols], held.at[:, cols], sems.at[c * 2 + k]))
    return out


def build_table(copies, params, table):
    zeros = jnp.zeros((64 - ROWS, LANES), F32)
    blocks = HALF // LANES // CHUNKS

    for c in range(CHUNKS):
        copies[c * 2].wait()
        copies[c * 2 + 1].wait()

        def block(b, _):
            first = pl.multiple_of((c * blocks + b) * LANES, LANES)
            both = jnp.concatenate(
                [params[:, pl.ds(first, LANES)], zeros, params[:, pl.ds(first + HALF, LANES)], zeros], 0
            )
            table[pl.ds(first, LANES), :] = both.T
            return 0

        lax.fori_loop(0, blocks, block, 0, unroll=8)


def gather_rows(index, table, rows, half_ref, turned):
    def some(step, _):
        for k in range(GROUP):
            for d in range(LANES):
                place = index[step * GROUP + k, d]
                rows[k * 128 + d : k * 128 + d + 1, :] = table[pl.ds(place, 1), :]
        for k in range(GROUP):
            r = step * GROUP + k
            both = rows[k * 128 : k * 128 + 128, :].T
            upper = half_ref[pl.ds(r, 1), :] > 0
            turned[pl.ds(pl.multiple_of(r * 64, 64), 64), :] = jnp.where(upper, both[64:], both[:64])
        return 0

    lax.fori_loop(0, SLOTS // GROUP, some, 0)


def split_index(sends_ref, row_ref, half_ref):
    turned = sends_ref[...]
    half_ref[...] = turned // HALF
    row_ref[...] = turned % HALF


def color_rows(basis, turned, color):
    def one(r, _):
        terms = basis[pl.ds(r, 16, stride=32), :]
        for ch in range(3):
            start = r * 64 + 6 + 16 * ch
            color[pl.ds(ch * 32 + r, 1), :] = 0.5 + jnp.sum(terms * turned[pl.ds(start, 16), :], axis=0, keepdims=True)
        return 0

    lax.fori_loop(0, SLOTS, one, 0, unroll=4)


def owner_message(turned, color, msg):
    geo = [turned[pl.ds(v, 32, stride=64), :] for v in range(6)]
    msg[:, 0, 0:128] = jnp.concatenate(geo[0:4], 0).T
    msg[:, 0, 128:256] = jnp.concatenate([geo[4], geo[5], color[0:32], color[32:64]], 0).T
    last = color[64:96]
    msg[:, 0, 256:384] = jnp.concatenate([last, last, last, last], 0).T


def entries_in_order(got, hot, slots, split, entry):
    zero = jnp.zeros((32, LANES), BF16)
    fine = {0: 288, 1: 320, 5: 352}
    for g, size in ((0, 128), (1, 128), (2, 32)):
        high, mid, low = split3(got[:, 0, g * 128 : g * 128 + 128].T[0:size])
        split[g * 128 : g * 128 + size, 0:128] = high
        split[g * 128 : g * 128 + size, 128:256] = mid
        for v, row in fine.items():
            if v // 4 == g:
                first = (v - g * 4) * 32
                split[row : row + 32, 0:128] = low[first : first + 32]
                split[row : row + 32, 128:256] = zero
    rows = iota((SLOTS, LANES), 0)

    def step(s, _):
        cols = hot[:, pl.ds(pl.multiple_of(s * WIDE * LANES, WIDE * LANES), WIDE * LANES)]
        picked = dot_nn(split[...], jnp.concatenate([cols, cols], 0))
        for k in range(WIDE):
            q = s * WIDE + k
            lane = slice(k * LANES, k * LANES + LANES)
            here = rows == slots[pl.ds(q, 1), :] % SLOTS
            for v in range(9):
                value = picked[v * 32 : v * 32 + 32, lane]
                if v in fine:
                    value = value + picked[fine[v] : fine[v] + 32, lane]
                kept = jnp.where(here, value, 0.0)
                entry[pl.ds(v * 32 + q, 1), :] = jnp.sum(kept, axis=0, keepdims=True)
        return 0

    lax.fori_loop(0, STEPS // WIDE, step, 0, unroll=UNROLL_ENTRY // WIDE)


def power_factors(entry, counts, factor):
    x = entry[0:32] - 8.0
    y = entry[32:64] - 8.0
    con_a = entry[64:96]
    con_b = entry[96:128]
    con_c = entry[128:160]
    logit = entry[160:192]
    position = iota((STEPS, LANES), 0) * 8 + iota((STEPS, LANES), 1) // 16
    tile = iota((STEPS, LANES), 1) % 16
    count = jnp.zeros((STEPS, LANES), I32)
    for t in range(16):
        count = jnp.where(tile == t, counts[t], count)
    live = position < count
    lin_x = con_a * x + con_b * y
    lin_y = con_b * x + con_c * y
    const = -0.5 * (x * lin_x + y * lin_y) - jnp.log(1.0 + jnp.exp(-logit))
    factors = [const, lin_x, lin_y, -0.5 * con_a, -con_b, -0.5 * con_c]
    for k, value in enumerate(factors):
        value = jnp.where(live, value * LOG2E, -1000.0 if k == 0 else 0.0)
        for p, part in enumerate(split3(value)):
            row = (p * 6 + k) * 32
            factor[row : row + 32, :] = part.astype(F32)
    for ch in range(3):
        for p, part in enumerate(split3(entry[192 + ch * 32 : 224 + ch * 32])):
            row = (18 + p * 3 + ch) * 32
            factor[row : row + 32, :] = part.astype(F32)
    factor[27 * 32 : 32 * 32, :] = jnp.zeros((5 * 32, LANES), F32)


def alphas_and_colors(factor, power, alpha, shade):
    def step(q, _):
        first = pl.multiple_of(q * LANES, LANES)
        left = factor[pl.ds(q, 32, stride=32), :].T.astype(BF16)
        out = dot_nn(left, power[...])
        alpha[pl.ds(first, LANES), :] = jnp.minimum(jnp.exp2(out[:, 0:256]), 0.99)
        shade[pl.ds(first, LANES), :] = out[:, 256:640]
        return 0

    lax.fori_loop(0, STEPS, step, 0, unroll=UNROLL_ALPHA)


def composite(alpha, shade, image):
    one = jnp.ones((16, LANES), F32)
    zero = jnp.zeros((16, LANES), F32)

    def step(q, state):
        through = list(state[0:2])
        total = list(state[2:8])
        for k in range(8):
            row = pl.ds(pl.multiple_of(q * LANES + k * 16, 16), 16)
            colors = [shade[row, ch * 128 : ch * 128 + 128] for ch in range(3)]
            for h in range(2):
                weight = alpha[row, h * 128 : h * 128 + 128] * through[h]
                through[h] = through[h] - weight
                for ch in range(3):
                    total[ch * 2 + h] = total[ch * 2 + h] + weight * colors[ch]
        return tuple(through + total)

    state = lax.fori_loop(0, STEPS, step, (one, one) + (zero,) * 6)
    for ch in range(3):
        for h in range(2):
            image[ch, :, h * 128 : h * 128 + 128] = state[2 + ch * 2 + h]


def weights_forward(alpha, weights):
    one = jnp.ones((16, LANES), F32)

    def step(q, through):
        through = list(through)
        for k in range(8):
            row = pl.ds(pl.multiple_of(q * LANES + k * 16, 16), 16)
            for h in range(2):
                weight = alpha[row, h * 128 : h * 128 + 128] * through[h]
                through[h] = through[h] - weight
                weights[row, h * 128 : h * 128 + 128] = weight
        return tuple(through)

    lax.fori_loop(0, STEPS, step, (one, one))


def backward(alpha, shade, weights, cot, moments, parts, parts_odd, against, sums):
    up = [cot[ch, :, h * 128 : h * 128 + 128] for ch in range(3) for h in range(2)]
    zero = jnp.zeros((16, LANES), F32)
    high, low = split2(cot[...].reshape(48, 256))
    against[...] = jnp.zeros((LANES, 1024), BF16)
    against[0:16, 0:512] = moments[...]
    against[16:64, 512:768] = high
    against[16:64, 768:1024] = high
    against[64:112, 512:768] = low
    own = iota((16, LANES), 0) == iota((16, LANES), 1) % 16

    def pull(s, behind, parts):
        behind = list(behind)
        for k in range(8 * BACK - 1, -1, -1):
            row = pl.ds(pl.multiple_of(s * BACK * LANES + k * 16, 16), 16)
            local = slice(k * 16, k * 16 + 16)
            colors = [shade[row, ch * 128 : ch * 128 + 128] for ch in range(3)]
            for h in range(2):
                opaque = alpha[row, h * 128 : h * 128 + 128]
                weight = weights[row, h * 128 : h * 128 + 128]
                value = up[h] * colors[0] + up[2 + h] * colors[1] + up[4 + h] * colors[2]
                ahead = value - behind[h]
                behind[h] = behind[h] + opaque * ahead
                pulled = jnp.where(opaque < 0.99, weight * ahead, 0.0)
                pieces = split2(pulled) + split2(weight)
                for p, piece in enumerate(pieces):
                    parts[local, p * 256 + h * 128 : p * 256 + h * 128 + 128] = piece
        return tuple(behind)

    def add_up(s, parts):
        totals = dot_nt(parts[...], against[...])
        for k in range(BACK):
            q = s * BACK + k
            turned = totals[k * 128 : k * 128 + 128].T
            for v in range(6):
                sums[pl.ds(v * 32 + q, 1), :] = turned[v : v + 1]
            for ch in range(3):
                first = 16 + ch * 16
                value = turned[first : first + 16] + turned[first + 48 : first + 64]
                kept = jnp.where(own, value, 0.0)
                sums[pl.ds((6 + ch) * 32 + q, 1), :] = jnp.sum(kept, axis=0, keepdims=True)

    last = STEPS // BACK - 1

    def step(j, behind):
        s = last - 1 - 2 * j
        behind = pull(s, behind, parts_odd)
        add_up(s + 1, parts)
        behind = pull(s - 1, behind, parts)
        add_up(s, parts_odd)
        return behind

    behind = lax.fori_loop(0, STEPS // BACK // 2 - 1, step, pull(last, (zero, zero), parts))
    pull(0, behind, parts_odd)
    add_up(1, parts)
    add_up(0, parts_odd)


def entry_gradients(entry, sums, grad):
    x = entry[0:32] - 8.0
    y = entry[32:64] - 8.0
    con_a = entry[64:96]
    con_b = entry[96:128]
    con_c = entry[128:160]
    fade = jnp.exp(-entry[160:192])
    s_0 = sums[0:32]
    s_x = sums[32:64]
    s_y = sums[64:96]
    d_x = s_x - x * s_0
    d_y = s_y - y * s_0
    d_xx = sums[96:128] - x * (s_x + d_x)
    d_xy = sums[128:160] - x * s_y - y * d_x
    d_yy = sums[160:192] - y * (s_y + d_y)
    values = [
        con_a * d_x + con_b * d_y,
        con_b * d_x + con_c * d_y,
        -0.5 * d_xx,
        -d_xy,
        -0.5 * d_yy,
        s_0 * (fade / (1.0 + fade)),
        sums[192:224],
        sums[224:256],
        sums[256:288],
    ]
    for v, value in enumerate(values):
        grad[v * 32 : v * 32 + 32, :] = value


def slots_in_order(grad, hot, slots, spread, msg):
    rows = iota((SLOTS, LANES), 0)

    def step(q, _):
        first = pl.multiple_of(q * LANES, LANES)
        here = rows == slots[pl.ds(q, 1), :] % SLOTS
        for v in range(9):
            value = grad[pl.ds(v * 32 + q, 1), :]
            high, low = split2(jnp.where(here, value, 0.0))
            spread[v * 32 : v * 32 + 32, pl.ds(first, LANES)] = high
            spread[288 + v * 32 : 320 + v * 32, pl.ds(first, LANES)] = low
        return 0

    lax.fori_loop(0, STEPS, step, 0, unroll=2)
    both = dot_nt(spread[...], hot[...])
    total = both[0:288] + both[288:576]
    msg[:, 0, 0:128] = total[0:128].T
    msg[:, 0, 128:256] = total[128:256].T
    last = total[256:288]
    msg[:, 0, 256:384] = jnp.concatenate([last, last, last, last], 0).T


def place_of(device):
    return (device // N_PIX, lax.rem(device, N_PIX))


def greet(me):
    barrier = pltpu.get_barrier_semaphore()

    def one(k, _):
        pl.semaphore_signal(barrier, inc=1, device_id=place_of(lax.rem(me + k, N_DEV)), device_id_type=MESH)
        return 0

    lax.fori_loop(1, N_DEV, one, 0, unroll=N_DEV - 1)


def await_greetings():
    pl.semaphore_wait(pltpu.get_barrier_semaphore(), N_DEV - 1)


def send_all(me, msg, got, send_sem, recv_sem):
    def one(k, _):
        there = lax.rem(me + k, N_DEV)
        pltpu.make_async_remote_copy(
            src_ref=msg.at[there],
            dst_ref=got.at[me],
            send_sem=send_sem,
            recv_sem=recv_sem,
            device_id=place_of(there),
            device_id_type=MESH,
        ).start()
        return 0

    lax.fori_loop(1, N_DEV, one, 0, unroll=N_DEV - 1)
    got[me] = msg[me]


def all_of(me, msg, got, send_sem, recv_sem):
    return pltpu.make_async_remote_copy(
        src_ref=msg.at[pl.ds(0, N_DEV - 1)],
        dst_ref=got.at[pl.ds(0, N_DEV - 1)],
        send_sem=send_sem,
        recv_sem=recv_sem,
        device_id=place_of(lax.rem(me + 1, N_DEV)),
        device_id_type=MESH,
    )


def main_kernel(
    params, lists_next, lists_cur, angles_next, angles_cur, counts_next, counts_cur,
    sends_next, sends_cur, cot, power, moments,
    image, returned, basis_cur,
    ask, asked, msg_cur, got_cur, msg_next, got_next, back, got_back,
    slots_next, slots_cur, hot_next, hot_cur, turned, mark,
    held_params, table, rows, rows_cur, rows_next, row_v, half_next, half_cur, row_next, row_cur, basis_next, color,
    split, entry, factor, alpha, shade, weights, parts, parts_odd, against, sums, grad, spread,
    send_sems, recv_sems, param_sems, index_sems,
):
    me = lax.axis_index("gauss") * N_PIX + lax.axis_index("pix")
    greet(me)
    copies = param_copies(params, held_params, param_sems)
    for copy in copies:
        copy.start()
    split_index(sends_cur, row_v.at[0], half_cur)
    split_index(sends_next, row_v.at[1], half_next)
    to_smem = [
        pltpu.make_async_copy(row_v.at[0], row_cur, index_sems.at[0]),
        pltpu.make_async_copy(row_v.at[1], row_next, index_sems.at[1]),
    ]
    for copy in to_smem:
        copy.start()
    order_lists(lists_next, turned, slots_next)
    owner_onehot(slots_next, hot_next)
    tiles_next = slot_tiles(slots_next, hot_next, mark)
    order_lists(lists_cur, turned, slots_cur)
    owner_onehot(slots_cur, hot_cur)
    tiles_cur = slot_tiles(slots_cur, hot_cur, mark)
    ask[:, 0, :] = angle_message(tiles_next, tiles_cur, angles_next, angles_cur)
    for copy in to_smem:
        copy.wait()
    build_table(copies, held_params, table)
    await_greetings()
    links = [
        (me, src, dst, send_sems.at[k], recv_sems.at[k])
        for k, (src, dst) in enumerate(((ask, asked), (msg_cur, got_cur), (msg_next, got_next), (back, got_back)))
    ]
    send_all(*links[0])
    gather_rows(row_cur, table, rows, half_cur, rows_cur)
    all_of(*links[0]).wait_recv()
    seen = asked[:, 0, :].T
    for k, term in enumerate(sh_terms(seen[64:96], seen[96:128])):
        basis_cur[k * 32 : k * 32 + 32, :] = term
    color_rows(basis_cur, rows_cur, color)
    owner_message(rows_cur, color, msg_cur)
    basis_cur[512:544, :] = jnp.zeros((32, LANES), F32)
    send_all(*links[1])
    for k, term in enumerate(sh_terms(seen[0:32], seen[32:64])):
        basis_next[k * 32 : k * 32 + 32, :] = term
    gather_rows(row_next, table, rows, half_next, rows_next)
    color_rows(basis_next, rows_next, color)
    owner_message(rows_next, color, msg_next)
    send_all(*links[2])
    all_of(*links[1]).wait_recv()
    entries_in_order(got_cur, hot_cur, slots_cur, split, entry)
    power_factors(entry, counts_cur, factor)
    alphas_and_colors(factor, power, alpha, shade)
    weights_forward(alpha, weights)
    backward(alpha, shade, weights, cot, moments, parts, parts_odd, against, sums)
    entry_gradients(entry, sums, grad)
    slots_in_order(grad, hot_cur, slots_cur, spread, back)
    send_all(*links[3])
    all_of(*links[2]).wait_recv()
    entries_in_order(got_next, hot_next, slots_next, split, entry)
    power_factors(entry, counts_next, factor)
    alphas_and_colors(factor, power, alpha, shade)
    composite(alpha, shade, image)
    all_of(*links[3]).wait_recv()
    for g in range(3):
        returned[g * 128 : g * 128 + 128, :] = got_back[:, 0, g * 128 : g * 128 + 128].T
    for link in links:
        all_of(*link).wait_send()


def scatter_kernel(turned, basis, sends, grads, row_v, half, row_s, total, piece, rows, out, sem, out_sems):
    split_index(sends, row_v, half)
    copy = pltpu.make_async_copy(row_v, row_s, sem)
    copy.start()

    def clear(b, _):
        total[pl.ds(pl.multiple_of(b * 512, 512), 512), :] = jnp.zeros((512, LANES), F32)
        return 0

    piece[...] = jnp.zeros((2, 64, LANES), F32)
    same_group = iota((LANES, LANES), 0) // 16 == iota((LANES, LANES), 1) // 16

    def prepare(r, k):
        piece[k, 0:6, :] = turned[pl.ds(r, 8, stride=32), :][0:6]
        terms = basis[pl.ds(r, 16, stride=32), :]
        for ch in range(3):
            piece[k, 6 + 16 * ch : 22 + 16 * ch, :] = terms * turned[pl.ds((6 + ch) * 32 + r, 1), :]
        upper = half[pl.ds(r, 1), :] > 0
        values = piece[k]
        both = jnp.concatenate([jnp.where(upper, 0.0, values), jnp.where(upper, values, 0.0)], 0)
        high, low = split2(both)
        name = jnp.broadcast_to(row_v[pl.ds(r, 1), :].astype(F32), (LANES, LANES))
        same = jnp.logical_and(name == name.T, same_group).astype(F32).astype(BF16)
        rows[k] = dot_nt(jnp.concatenate([same, same], 1), jnp.concatenate([high, low], 1))

    def add(r, k):
        for g in range(8):
            places = [row_s[r, g * 16 + u] for u in range(16)]
            olds = [total[pl.ds(places[u], 1), :] for u in range(16)]
            for u in range(16):
                total[pl.ds(places[u], 1), :] = olds[u] + rows[k, g * 16 + u : g * 16 + u + 1, :]

    prepare(0, 0)
    lax.fori_loop(0, HALF // 512, clear, 0)
    copy.wait()

    def slots(s, _):
        for k in range(PAIR):
            prepare(lax.rem(s * PAIR + k + 1, SLOTS), (k + 1) % 2)
            add(s * PAIR + k, k % 2)
        return 0

    lax.fori_loop(0, SLOTS // PAIR, slots, 0)

    width = HALF // CHUNKS
    writes = []
    for c in range(CHUNKS):
        def block(b, _):
            first = pl.multiple_of(c * width + b * LANES, LANES)
            both = total[pl.ds(first, LANES), :].T
            out[:, pl.ds(first, LANES)] = both[0:ROWS]
            out[:, pl.ds(first + HALF, LANES)] = both[64 : 64 + ROWS]
            return 0

        lax.fori_loop(0, width // LANES, block, 0, unroll=8)
        for k in range(2):
            cols = pl.ds(k * HALF + c * width, width)
            write = pltpu.make_async_copy(out.at[:, cols], grads.at[:, cols], out_sems.at[c * 2 + k])
            write.start()
            writes.append(write)
    for write in writes:
        write.wait()


VM = pl.BlockSpec(memory_space=pltpu.VMEM)
SM = pl.BlockSpec(memory_space=pltpu.SMEM)
PARAMS = pltpu.CompilerParams(vmem_limit_bytes=VMEM_LIMIT)


def shape(dims, dtype=F32):
    return jax.ShapeDtypeStruct(dims, dtype)


def body(params, angles_next, angles_cur, lists_next, lists_cur, counts_next, counts_cur, sends_next, sends_cur, cotangent):
    power, moments = pixel_tables()
    dense = (STEPS, LANES)
    wide = pltpu.VMEM((N_DEV, 1, 384), F32)
    image, returned, basis = pl.pallas_call(
        main_kernel,
        out_shape=(shape((3, 16, 256)), shape((384, LANES)), shape((544, LANES))),
        in_specs=[pl.BlockSpec(memory_space=pl.ANY), VM, VM, SM, SM, SM, SM, VM, VM, VM, VM, VM],
        out_specs=(VM,) * 3,
        scratch_shapes=[
            pltpu.VMEM((N_DEV, 1, 128), F32),
            pltpu.VMEM((N_DEV, 1, 128), F32),
            wide, wide, wide, wide, wide, wide,
            pltpu.VMEM(dense, I32),
            pltpu.VMEM(dense, I32),
            pltpu.VMEM((N_DEV, 4096), BF16),
            pltpu.VMEM((N_DEV, 4096), BF16),
            pltpu.VMEM((264, LANES), I32),
            pltpu.VMEM((SLOTS, 4096), BF16),
            pltpu.VMEM((ROWS, GAUSS), F32),
            pltpu.VMEM((HALF, LANES), F32),
            pltpu.VMEM((GROUP * LANES, LANES), F32),
            pltpu.VMEM((SLOTS * 64 + 8, LANES), F32),
            pltpu.VMEM((SLOTS * 64 + 8, LANES), F32),
            pltpu.VMEM((2,) + dense, I32),
            pltpu.VMEM(dense, I32),
            pltpu.VMEM(dense, I32),
            pltpu.SMEM(dense, I32),
            pltpu.SMEM(dense, I32),
            pltpu.VMEM((544, LANES), F32),
            pltpu.VMEM((96, LANES), F32),
            pltpu.VMEM((384, 256), BF16),
            pltpu.VMEM((288, LANES), F32),
            pltpu.VMEM((1056, LANES), F32),
            pltpu.VMEM((4096, 256), F32),
            pltpu.VMEM((4096, 384), F32),
            pltpu.VMEM((4096, 256), F32),
            pltpu.VMEM((BACK * LANES, 1024), BF16),
            pltpu.VMEM((BACK * LANES, 1024), BF16),
            pltpu.VMEM((LANES, 1024), BF16),
            pltpu.VMEM((288, LANES), F32),
            pltpu.VMEM((288, LANES), F32),
            pltpu.VMEM((576, 4096), BF16),
            pltpu.SemaphoreType.DMA((4,)),
            pltpu.SemaphoreType.DMA((4,)),
            pltpu.SemaphoreType.DMA((2 * CHUNKS,)),
            pltpu.SemaphoreType.DMA((2,)),
        ],
        compiler_params=pltpu.CompilerParams(
            vmem_limit_bytes=VMEM_LIMIT, collective_id=0, has_side_effects=True
        ),
        name="main",
    )(params, lists_next, lists_cur, jnp.transpose(angles_next), jnp.transpose(angles_cur), counts_next, counts_cur,
      jnp.transpose(sends_next[0]), jnp.transpose(sends_cur[0]), jnp.transpose(cotangent, (1, 0, 2)), power, moments)
    grads = pl.pallas_call(
        scatter_kernel,
        out_shape=shape((ROWS, GAUSS)),
        in_specs=[VM] * 3,
        out_specs=pl.BlockSpec(memory_space=pl.ANY),
        scratch_shapes=[
            pltpu.VMEM(dense, I32),
            pltpu.VMEM(dense, I32),
            pltpu.SMEM(dense, I32),
            pltpu.VMEM((HALF, LANES), F32),
            pltpu.VMEM((2, 64, LANES), F32),
            pltpu.VMEM((2, LANES, LANES), F32),
            pltpu.VMEM((ROWS, GAUSS), F32),
            pltpu.SemaphoreType.DMA,
            pltpu.SemaphoreType.DMA((2 * CHUNKS,)),
        ],
        compiler_params=PARAMS,
        name="scatter",
    )(returned, basis, jnp.transpose(sends_cur[0]))
    return jnp.transpose(image, (1, 0, 2)), grads


def solution(mesh):
    both = ("gauss", "pix")
    placed = (
        P(None, both),
        P(both, None),
        P(both, None),
        P(both, None),
        P(both, None),
        P(both),
        P(both),
        P(both, None, None),
        P(both, None, None),
        P(both, None, None),
    )
    return jax.shard_map(
        body,
        mesh=mesh,
        in_specs=placed,
        out_specs=(P(both, None, None), P(None, both)),
        check_vma=False,
    )
```

```python
import jax
import jax.numpy as jnp
import numpy as np
from jax import lax
from jax.experimental import pallas as pl
from jax.experimental.pallas import tpu as pltpu
from jax.sharding import PartitionSpec as P

F32 = jnp.float32
BF16 = jnp.bfloat16
I32 = jnp.int32
MESH = pl.DeviceIdType.MESH
N_DEV = 128
N_PIX = 32
SLOTS = 32
GAUSS = 16384
HALF = 8192
CHUNKS = 4
UNROLL_ENTRY = 8
BACK = 4
PAIR = 8
WIDE = 2
UNROLL_ALPHA = 8
GROUP = 8
ROWS = 54
LANES = 128
STEPS = 32
LOG2E = 1.4426950408889634
VMEM_LIMIT = 56 * 2**20


def iota(shape, dim):
    return lax.broadcasted_iota(I32, shape, dim)


def dot_nn(a, b):
    return lax.dot_general(a, b, (((1,), (0,)), ((), ())), preferred_element_type=F32)


def dot_nt(a, b):
    return lax.dot_general(a, b, (((1,), (1,)), ((), ())), preferred_element_type=F32)


def split2(x):
    high = x.astype(BF16)
    low = (x - high.astype(F32)).astype(BF16)
    return high, low


def split3(x):
    high = x.astype(BF16)
    rest = x - high.astype(F32)
    mid = rest.astype(BF16)
    low = (rest - mid.astype(F32)).astype(BF16)
    return high, mid, low


def pixel_tables():
    pixels = np.arange(256)
    qx = (pixels % 16) - 7.5
    qy = (pixels // 16) - 7.5
    mono = np.stack([np.ones(256), qx, qy, qx * qx, qx * qy, qy * qy], 0)
    power = np.zeros((32, 640), np.float32)
    for part in range(3):
        power[part * 6 : part * 6 + 6, :256] = mono
        for ch in range(3):
            power[18 + part * 3 + ch, 256 + 128 * ch : 384 + 128 * ch] = 1.0
    moments = np.zeros((16, 512), np.float32)
    moments[:6, :256] = mono
    moments[:6, 256:] = mono
    return jnp.asarray(power, BF16), jnp.asarray(moments, BF16)


def order_lists(lists_ref, turned, slots_ref):
    turned[0:256, 0:16] = lists_ref[...].T
    lane_group = iota((STEPS, LANES), 1) // 16
    out = jnp.zeros((STEPS, LANES), I32)
    for k in range(8):
        piece = pltpu.roll(turned[pl.ds(k, STEPS, stride=8), :], 16 * k, 1) if k else turned[pl.ds(0, STEPS, stride=8), :]
        out = jnp.where(lane_group == k, piece, out)
    slots_ref[...] = out


def owner_onehot(slots_ref, hot_ref):
    rows = iota((N_DEV, LANES), 0)
    for q in range(STEPS):
        owner = slots_ref[q : q + 1, :] // SLOTS
        hot_ref[:, q * LANES : (q + 1) * LANES] = (rows == owner).astype(F32).astype(BF16)


def slot_tiles(slots_ref, hot_ref, mark_ref):
    rows = iota((SLOTS, LANES), 0)
    tile = (iota((SLOTS, LANES), 1) % 16).astype(F32)
    for q in range(STEPS):
        place = slots_ref[q : q + 1, :] % SLOTS
        mark_ref[:, q * LANES : (q + 1) * LANES] = jnp.where(rows == place, tile, 0.0).astype(BF16)
    return dot_nt(hot_ref[...], mark_ref[...])


def angle_message(tiles_next, tiles_cur, angles_next, angles_cur):
    tiles = jnp.concatenate([tiles_next, tiles_next, tiles_cur, tiles_cur], 1)
    region = iota((1, LANES), 1) // 32
    out = jnp.zeros((N_DEV, LANES), F32)
    for t in range(16):
        row = jnp.where(
            region < 2,
            jnp.where(region == 0, angles_next[0, t], angles_next[1, t]),
            jnp.where(region == 2, angles_cur[0, t], angles_cur[1, t]),
        )
        out = jnp.where(tiles == float(t), row, out)
    return out


def sh_terms(theta, azimuth):
    sin_t = jnp.sin(theta)
    dir_x = sin_t * jnp.cos(azimuth)
    dir_y = sin_t * jnp.sin(azimuth)
    dir_z = jnp.cos(theta)
    sq_x = dir_x * dir_x
    sq_y = dir_y * dir_y
    sq_z = dir_z * dir_z
    return [
        0.28209479177387814 * jnp.ones_like(dir_x),
        -0.4886025119029199 * dir_y,
        0.4886025119029199 * dir_z,
        -0.4886025119029199 * dir_x,
        1.0925484305920792 * dir_x * dir_y,
        -1.0925484305920792 * dir_y * dir_z,
        0.31539156525252005 * (2.0 * sq_z - sq_x - sq_y),
        -1.0925484305920792 * dir_x * dir_z,
        0.5462742152960396 * (sq_x - sq_y),
        -0.5900435899266435 * dir_y * (3.0 * sq_x - sq_y),
        2.890611442640554 * dir_x * dir_y * dir_z,
        -0.4570457994644658 * dir_y * (4.0 * sq_z - sq_x - sq_y),
        0.3731763325901154 * dir_z * (2.0 * sq_z - 3.0 * sq_x - 3.0 * sq_y),
        -0.4570457994644658 * dir_x * (4.0 * sq_z - sq_x - sq_y),
        1.445305721320277 * dir_z * (sq_x - sq_y),
        -0.5900435899266435 * dir_x * (sq_x - 3.0 * sq_y),
    ]


def param_copies(params, held, sems):
    width = HALF // CHUNKS
    out = []
    for c in range(CHUNKS):
        for k in range(2):
            cols = pl.ds(k * HALF + c * width, width)
            out.append(pltpu.make_async_copy(params.at[:, cols], held.at[:, cols], sems.at[c * 2 + k]))
    return out


def build_table(copies, params, table):
    zeros = jnp.zeros((64 - ROWS, LANES), F32)
    blocks = HALF // LANES // CHUNKS

    for c in range(CHUNKS):
        copies[c * 2].wait()
        copies[c * 2 + 1].wait()

        def block(b, _):
            first = pl.multiple_of((c * blocks + b) * LANES, LANES)
            both = jnp.concatenate(
                [params[:, pl.ds(first, LANES)], zeros, params[:, pl.ds(first + HALF, LANES)], zeros], 0
            )
            table[pl.ds(first, LANES), :] = both.T
            return 0

        lax.fori_loop(0, blocks, block, 0, unroll=8)


def gather_rows(index, table, rows, half_ref, turned):
    def some(step, _):
        for k in range(GROUP):
            for d in range(LANES):
                place = index[step * GROUP + k, d]
                rows[k * 128 + d : k * 128 + d + 1, :] = table[pl.ds(place, 1), :]
        for k in range(GROUP):
            r = step * GROUP + k
            both = rows[k * 128 : k * 128 + 128, :].T
            upper = half_ref[pl.ds(r, 1), :] > 0
            turned[pl.ds(pl.multiple_of(r * 64, 64), 64), :] = jnp.where(upper, both[64:], both[:64])
        return 0

    lax.fori_loop(0, SLOTS // GROUP, some, 0)


def split_index(sends_ref, row_ref, half_ref):
    turned = sends_ref[...]
    half_ref[...] = turned // HALF
    row_ref[...] = turned % HALF


def color_rows(basis, turned, color):
    def one(r, _):
        terms = basis[pl.ds(r, 16, stride=32), :]
        for ch in range(3):
            start = r * 64 + 6 + 16 * ch
            color[pl.ds(ch * 32 + r, 1), :] = 0.5 + jnp.sum(terms * turned[pl.ds(start, 16), :], axis=0, keepdims=True)
        return 0

    lax.fori_loop(0, SLOTS, one, 0, unroll=4)


def owner_message(turned, color, msg):
    geo = [turned[pl.ds(v, 32, stride=64), :] for v in range(6)]
    msg[:, 0, 0:128] = jnp.concatenate(geo[0:4], 0).T
    msg[:, 0, 128:256] = jnp.concatenate([geo[4], geo[5], color[0:32], color[32:64]], 0).T
    last = color[64:96]
    msg[:, 0, 256:384] = jnp.concatenate([last, last, last, last], 0).T


def entries_in_order(got, hot, slots, split, entry):
    zero = jnp.zeros((32, LANES), BF16)
    fine = {0: 288, 1: 320, 5: 352}
    for g, size in ((0, 128), (1, 128), (2, 32)):
        high, mid, low = split3(got[:, 0, g * 128 : g * 128 + 128].T[0:size])
        split[g * 128 : g * 128 + size, 0:128] = high
        split[g * 128 : g * 128 + size, 128:256] = mid
        for v, row in fine.items():
            if v // 4 == g:
                first = (v - g * 4) * 32
                split[row : row + 32, 0:128] = low[first : first + 32]
                split[row : row + 32, 128:256] = zero
    rows = iota((SLOTS, LANES), 0)

    def step(s, _):
        cols = hot[:, pl.ds(pl.multiple_of(s * WIDE * LANES, WIDE * LANES), WIDE * LANES)]
        picked = dot_nn(split[...], jnp.concatenate([cols, cols], 0))
        for k in range(WIDE):
            q = s * WIDE + k
            lane = slice(k * LANES, k * LANES + LANES)
            here = rows == slots[pl.ds(q, 1), :] % SLOTS
            for v in range(9):
                value = picked[v * 32 : v * 32 + 32, lane]
                if v in fine:
                    value = value + picked[fine[v] : fine[v] + 32, lane]
                kept = jnp.where(here, value, 0.0)
                entry[pl.ds(v * 32 + q, 1), :] = jnp.sum(kept, axis=0, keepdims=True)
        return 0

    lax.fori_loop(0, STEPS // WIDE, step, 0, unroll=UNROLL_ENTRY // WIDE)


def power_factors(entry, counts, factor):
    x = entry[0:32] - 8.0
    y = entry[32:64] - 8.0
    con_a = entry[64:96]
    con_b = entry[96:128]
    con_c = entry[128:160]
    logit = entry[160:192]
    position = iota((STEPS, LANES), 0) * 8 + iota((STEPS, LANES), 1) // 16
    tile = iota((STEPS, LANES), 1) % 16
    count = jnp.zeros((STEPS, LANES), I32)
    for t in range(16):
        count = jnp.where(tile == t, counts[t], count)
    live = position < count
    lin_x = con_a * x + con_b * y
    lin_y = con_b * x + con_c * y
    const = -0.5 * (x * lin_x + y * lin_y) - jnp.log(1.0 + jnp.exp(-logit))
    factors = [const, lin_x, lin_y, -0.5 * con_a, -con_b, -0.5 * con_c]
    for k, value in enumerate(factors):
        value = jnp.where(live, value * LOG2E, -1000.0 if k == 0 else 0.0)
        for p, part in enumerate(split3(value)):
            row = (p * 6 + k) * 32
            factor[row : row + 32, :] = part.astype(F32)
    for ch in range(3):
        for p, part in enumerate(split3(entry[192 + ch * 32 : 224 + ch * 32])):
            row = (18 + p * 3 + ch) * 32
            factor[row : row + 32, :] = part.astype(F32)
    factor[27 * 32 : 32 * 32, :] = jnp.zeros((5 * 32, LANES), F32)


def alphas_and_colors(factor, power, alpha, shade):
    def step(q, _):
        first = pl.multiple_of(q * LANES, LANES)
        left = factor[pl.ds(q, 32, stride=32), :].T.astype(BF16)
        out = dot_nn(left, power[...])
        alpha[pl.ds(first, LANES), :] = jnp.minimum(jnp.exp2(out[:, 0:256]), 0.99)
        shade[pl.ds(first, LANES), :] = out[:, 256:640]
        return 0

    lax.fori_loop(0, STEPS, step, 0, unroll=UNROLL_ALPHA)


def composite(alpha, shade, image):
    one = jnp.ones((16, LANES), F32)
    zero = jnp.zeros((16, LANES), F32)

    def step(q, state):
        through = list(state[0:2])
        total = list(state[2:8])
        for k in range(8):
            row = pl.ds(pl.multiple_of(q * LANES + k * 16, 16), 16)
            colors = [shade[row, ch * 128 : ch * 128 + 128] for ch in range(3)]
            for h in range(2):
                weight = alpha[row, h * 128 : h * 128 + 128] * through[h]
                through[h] = through[h] - weight
                for ch in range(3):
                    total[ch * 2 + h] = total[ch * 2 + h] + weight * colors[ch]
        return tuple(through + total)

    state = lax.fori_loop(0, STEPS, step, (one, one) + (zero,) * 6)
    for ch in range(3):
        for h in range(2):
            image[ch, :, h * 128 : h * 128 + 128] = state[2 + ch * 2 + h]


def weights_forward(alpha, weights):
    one = jnp.ones((16, LANES), F32)

    def step(q, through):
        through = list(through)
        for k in range(8):
            row = pl.ds(pl.multiple_of(q * LANES + k * 16, 16), 16)
            for h in range(2):
                weight = alpha[row, h * 128 : h * 128 + 128] * through[h]
                through[h] = through[h] - weight
                weights[row, h * 128 : h * 128 + 128] = weight
        return tuple(through)

    lax.fori_loop(0, STEPS, step, (one, one))


def backward(alpha, shade, weights, cot, moments, parts, parts_odd, against, sums):
    up = [cot[ch, :, h * 128 : h * 128 + 128] for ch in range(3) for h in range(2)]
    zero = jnp.zeros((16, LANES), F32)
    high, low = split2(cot[...].reshape(48, 256))
    against[...] = jnp.zeros((LANES, 1024), BF16)
    against[0:16, 0:512] = moments[...]
    against[16:64, 512:768] = high
    against[16:64, 768:1024] = high
    against[64:112, 512:768] = low
    own = iota((16, LANES), 0) == iota((16, LANES), 1) % 16

    def pull(s, behind, parts):
        behind = list(behind)
        for k in range(8 * BACK - 1, -1, -1):
            row = pl.ds(pl.multiple_of(s * BACK * LANES + k * 16, 16), 16)
            local = slice(k * 16, k * 16 + 16)
            colors = [shade[row, ch * 128 : ch * 128 + 128] for ch in range(3)]
            for h in range(2):
                opaque = alpha[row, h * 128 : h * 128 + 128]
                weight = weights[row, h * 128 : h * 128 + 128]
                value = up[h] * colors[0] + up[2 + h] * colors[1] + up[4 + h] * colors[2]
                ahead = value - behind[h]
                behind[h] = behind[h] + opaque * ahead
                pulled = jnp.where(opaque < 0.99, weight * ahead, 0.0)
                pieces = split2(pulled) + split2(weight)
                for p, piece in enumerate(pieces):
                    parts[local, p * 256 + h * 128 : p * 256 + h * 128 + 128] = piece
        return tuple(behind)

    def add_up(s, parts):
        totals = dot_nt(parts[...], against[...])
        for k in range(BACK):
            q = s * BACK + k
            turned = totals[k * 128 : k * 128 + 128].T
            for v in range(6):
                sums[pl.ds(v * 32 + q, 1), :] = turned[v : v + 1]
            for ch in range(3):
                first = 16 + ch * 16
                value = turned[first : first + 16] + turned[first + 48 : first + 64]
                kept = jnp.where(own, value, 0.0)
                sums[pl.ds((6 + ch) * 32 + q, 1), :] = jnp.sum(kept, axis=0, keepdims=True)

    last = STEPS // BACK - 1

    def step(j, behind):
        s = last - 1 - 2 * j
        behind = pull(s, behind, parts_odd)
        add_up(s + 1, parts)
        behind = pull(s - 1, behind, parts)
        add_up(s, parts_odd)
        return behind

    behind = lax.fori_loop(0, STEPS // BACK // 2 - 1, step, pull(last, (zero, zero), parts))
    pull(0, behind, parts_odd)
    add_up(1, parts)
    add_up(0, parts_odd)


def entry_gradients(entry, sums, grad):
    x = entry[0:32] - 8.0
    y = entry[32:64] - 8.0
    con_a = entry[64:96]
    con_b = entry[96:128]
    con_c = entry[128:160]
    fade = jnp.exp(-entry[160:192])
    s_0 = sums[0:32]
    s_x = sums[32:64]
    s_y = sums[64:96]
    d_x = s_x - x * s_0
    d_y = s_y - y * s_0
    d_xx = sums[96:128] - x * (s_x + d_x)
    d_xy = sums[128:160] - x * s_y - y * d_x
    d_yy = sums[160:192] - y * (s_y + d_y)
    values = [
        con_a * d_x + con_b * d_y,
        con_b * d_x + con_c * d_y,
        -0.5 * d_xx,
        -d_xy,
        -0.5 * d_yy,
        s_0 * (fade / (1.0 + fade)),
        sums[192:224],
        sums[224:256],
        sums[256:288],
    ]
    for v, value in enumerate(values):
        grad[v * 32 : v * 32 + 32, :] = value


def slots_in_order(grad, hot, slots, spread, spread_odd, folded, msg):
    rows = iota((SLOTS, LANES), 0)

    def build(c, buffer):
        for k in range(4):
            q = c * 4 + k
            lane = slice(k * LANES, k * LANES + LANES)
            here = rows == slots[pl.ds(q, 1), :] % SLOTS
            for v in range(9):
                value = grad[pl.ds(v * 32 + q, 1), :]
                high, low = split2(jnp.where(here, value, 0.0))
                buffer[v * 32 : v * 32 + 32, lane] = high
                buffer[288 + v * 32 : 320 + v * 32, lane] = low

    def fold(c, buffer):
        both = dot_nt(buffer[...], hot[:, pl.ds(pl.multiple_of(c * 512, 512), 512)])
        folded[...] += both[0:288] + both[288:576]

    def step(j, _):
        build(2 * j + 1, spread_odd)
        fold(2 * j, spread)
        build(2 * j + 2, spread)
        fold(2 * j + 1, spread_odd)
        return 0

    folded[...] = jnp.zeros((288, LANES), F32)
    build(0, spread)
    lax.fori_loop(0, STEPS // 8 - 1, step, 0)
    build(STEPS // 4 - 1, spread_odd)
    fold(STEPS // 4 - 2, spread)
    fold(STEPS // 4 - 1, spread_odd)
    msg[:, 0, 0:128] = folded[0:128, :].T
    msg[:, 0, 128:256] = folded[128:256, :].T
    last = folded[256:288, :]
    msg[:, 0, 256:384] = jnp.concatenate([last, last, last, last], 0).T


def place_of(device):
    return (device // N_PIX, lax.rem(device, N_PIX))


def greet(me):
    barrier = pltpu.get_barrier_semaphore()

    def one(k, _):
        pl.semaphore_signal(barrier, inc=1, device_id=place_of(lax.rem(me + k, N_DEV)), device_id_type=MESH)
        return 0

    lax.fori_loop(1, N_DEV, one, 0, unroll=N_DEV - 1)


def await_greetings():
    pl.semaphore_wait(pltpu.get_barrier_semaphore(), N_DEV - 1)


def send_all(me, msg, got, send_sem, recv_sem):
    def one(k, _):
        there = lax.rem(me + k, N_DEV)
        pltpu.make_async_remote_copy(
            src_ref=msg.at[there],
            dst_ref=got.at[me],
            send_sem=send_sem,
            recv_sem=recv_sem,
            device_id=place_of(there),
            device_id_type=MESH,
        ).start()
        return 0

    lax.fori_loop(1, N_DEV, one, 0, unroll=N_DEV - 1)
    got[me] = msg[me]


def all_of(me, msg, got, send_sem, recv_sem):
    return pltpu.make_async_remote_copy(
        src_ref=msg.at[pl.ds(0, N_DEV - 1)],
        dst_ref=got.at[pl.ds(0, N_DEV - 1)],
        send_sem=send_sem,
        recv_sem=recv_sem,
        device_id=place_of(lax.rem(me + 1, N_DEV)),
        device_id_type=MESH,
    )


def main_kernel(
    params, lists_next, lists_cur, angles_next, angles_cur, counts_next, counts_cur,
    sends_next, sends_cur, cot, power, moments,
    image, returned, basis_cur,
    ask, asked, msg_cur, got_cur, msg_next, got_next, back, got_back,
    slots_next, slots_cur, hot_next, hot_cur, turned, mark,
    held_params, table, rows, rows_cur, rows_next, row_v, half_next, half_cur, row_next, row_cur, basis_next, color,
    split, entry, factor, alpha, shade, weights, parts, parts_odd, against, sums, grad, spread, spread_odd, folded,
    send_sems, recv_sems, param_sems, index_sems,
):
    me = lax.axis_index("gauss") * N_PIX + lax.axis_index("pix")
    greet(me)
    copies = param_copies(params, held_params, param_sems)
    for copy in copies:
        copy.start()
    split_index(sends_cur, row_v.at[0], half_cur)
    split_index(sends_next, row_v.at[1], half_next)
    to_smem = [
        pltpu.make_async_copy(row_v.at[0], row_cur, index_sems.at[0]),
        pltpu.make_async_copy(row_v.at[1], row_next, index_sems.at[1]),
    ]
    for copy in to_smem:
        copy.start()
    order_lists(lists_next, turned, slots_next)
    owner_onehot(slots_next, hot_next)
    tiles_next = slot_tiles(slots_next, hot_next, mark)
    order_lists(lists_cur, turned, slots_cur)
    owner_onehot(slots_cur, hot_cur)
    tiles_cur = slot_tiles(slots_cur, hot_cur, mark)
    ask[:, 0, :] = angle_message(tiles_next, tiles_cur, angles_next, angles_cur)
    for copy in to_smem:
        copy.wait()
    build_table(copies, held_params, table)
    await_greetings()
    links = [
        (me, src, dst, send_sems.at[k], recv_sems.at[k])
        for k, (src, dst) in enumerate(((ask, asked), (msg_cur, got_cur), (msg_next, got_next), (back, got_back)))
    ]
    send_all(*links[0])
    gather_rows(row_cur, table, rows, half_cur, rows_cur)
    all_of(*links[0]).wait_recv()
    seen = asked[:, 0, :].T
    for k, term in enumerate(sh_terms(seen[64:96], seen[96:128])):
        basis_cur[k * 32 : k * 32 + 32, :] = term
    color_rows(basis_cur, rows_cur, color)
    owner_message(rows_cur, color, msg_cur)
    basis_cur[512:544, :] = jnp.zeros((32, LANES), F32)
    send_all(*links[1])
    for k, term in enumerate(sh_terms(seen[0:32], seen[32:64])):
        basis_next[k * 32 : k * 32 + 32, :] = term
    gather_rows(row_next, table, rows, half_next, rows_next)
    color_rows(basis_next, rows_next, color)
    owner_message(rows_next, color, msg_next)
    send_all(*links[2])
    all_of(*links[1]).wait_recv()
    entries_in_order(got_cur, hot_cur, slots_cur, split, entry)
    power_factors(entry, counts_cur, factor)
    alphas_and_colors(factor, power, alpha, shade)
    weights_forward(alpha, weights)
    backward(alpha, shade, weights, cot, moments, parts, parts_odd, against, sums)
    entry_gradients(entry, sums, grad)
    slots_in_order(grad, hot_cur, slots_cur, spread, spread_odd, folded, back)
    send_all(*links[3])
    all_of(*links[2]).wait_recv()
    entries_in_order(got_next, hot_next, slots_next, split, entry)
    power_factors(entry, counts_next, factor)
    alphas_and_colors(factor, power, alpha, shade)
    composite(alpha, shade, image)
    all_of(*links[3]).wait_recv()
    for g in range(3):
        returned[g * 128 : g * 128 + 128, :] = got_back[:, 0, g * 128 : g * 128 + 128].T
    for link in links:
        all_of(*link).wait_send()


def scatter_kernel(turned, basis, sends, drawn, grads, image, row_v, half, row_s, total, piece, rows, out, sem, image_sem, out_sems):
    handed = pltpu.make_async_copy(drawn, image, image_sem)
    handed.start()
    split_index(sends, row_v, half)
    copy = pltpu.make_async_copy(row_v, row_s, sem)
    copy.start()

    def clear(b, _):
        total[pl.ds(pl.multiple_of(b * 512, 512), 512), :] = jnp.zeros((512, LANES), F32)
        return 0

    piece[...] = jnp.zeros((2, 64, LANES), F32)
    same_group = iota((LANES, LANES), 0) // 16 == iota((LANES, LANES), 1) // 16

    def prepare(r, k):
        piece[k, 0:6, :] = turned[pl.ds(r, 8, stride=32), :][0:6]
        terms = basis[pl.ds(r, 16, stride=32), :]
        for ch in range(3):
            piece[k, 6 + 16 * ch : 22 + 16 * ch, :] = terms * turned[pl.ds((6 + ch) * 32 + r, 1), :]
        upper = half[pl.ds(r, 1), :] > 0
        values = piece[k]
        both = jnp.concatenate([jnp.where(upper, 0.0, values), jnp.where(upper, values, 0.0)], 0)
        high, low = split2(both)
        name = jnp.broadcast_to(row_v[pl.ds(r, 1), :].astype(F32), (LANES, LANES))
        same = jnp.logical_and(name == name.T, same_group).astype(F32).astype(BF16)
        rows[k] = dot_nt(jnp.concatenate([same, same], 1), jnp.concatenate([high, low], 1))

    def add(r, k):
        for g in range(8):
            places = [row_s[r, g * 16 + u] for u in range(16)]
            olds = [total[pl.ds(places[u], 1), :] for u in range(16)]
            for u in range(16):
                total[pl.ds(places[u], 1), :] = olds[u] + rows[k, g * 16 + u : g * 16 + u + 1, :]

    prepare(0, 0)
    lax.fori_loop(0, HALF // 512, clear, 0)
    copy.wait()

    def slots(s, _):
        for k in range(PAIR):
            prepare(lax.rem(s * PAIR + k + 1, SLOTS), (k + 1) % 2)
            add(s * PAIR + k, k % 2)
        return 0

    lax.fori_loop(0, SLOTS // PAIR, slots, 0)

    width = HALF // CHUNKS
    writes = []
    for c in range(CHUNKS):
        def block(b, _):
            first = pl.multiple_of(c * width + b * LANES, LANES)
            both = total[pl.ds(first, LANES), :].T
            out[:, pl.ds(first, LANES)] = both[0:ROWS]
            out[:, pl.ds(first + HALF, LANES)] = both[64 : 64 + ROWS]
            return 0

        lax.fori_loop(0, width // LANES, block, 0, unroll=8)
        for k in range(2):
            cols = pl.ds(k * HALF + c * width, width)
            write = pltpu.make_async_copy(out.at[:, cols], grads.at[:, cols], out_sems.at[c * 2 + k])
            write.start()
            writes.append(write)
    for write in writes:
        write.wait()
    handed.wait()


VM = pl.BlockSpec(memory_space=pltpu.VMEM)
SM = pl.BlockSpec(memory_space=pltpu.SMEM)
PARAMS = pltpu.CompilerParams(vmem_limit_bytes=VMEM_LIMIT)


def shape(dims, dtype=F32):
    return jax.ShapeDtypeStruct(dims, dtype)


def body(params, angles_next, angles_cur, lists_next, lists_cur, counts_next, counts_cur, sends_next, sends_cur, cotangent):
    power, moments = pixel_tables()
    dense = (STEPS, LANES)
    wide = pltpu.VMEM((N_DEV, 1, 384), F32)
    image, returned, basis = pl.pallas_call(
        main_kernel,
        out_shape=(shape((3, 16, 256)), shape((384, LANES)), shape((544, LANES))),
        in_specs=[pl.BlockSpec(memory_space=pl.ANY), VM, VM, SM, SM, SM, SM, VM, VM, VM, VM, VM],
        out_specs=(VM,) * 3,
        scratch_shapes=[
            pltpu.VMEM((N_DEV, 1, 128), F32),
            pltpu.VMEM((N_DEV, 1, 128), F32),
            wide, wide, wide, wide, wide, wide,
            pltpu.VMEM(dense, I32),
            pltpu.VMEM(dense, I32),
            pltpu.VMEM((N_DEV, 4096), BF16),
            pltpu.VMEM((N_DEV, 4096), BF16),
            pltpu.VMEM((264, LANES), I32),
            pltpu.VMEM((SLOTS, 4096), BF16),
            pltpu.VMEM((ROWS, GAUSS), F32),
            pltpu.VMEM((HALF, LANES), F32),
            pltpu.VMEM((GROUP * LANES, LANES), F32),
            pltpu.VMEM((SLOTS * 64 + 8, LANES), F32),
            pltpu.VMEM((SLOTS * 64 + 8, LANES), F32),
            pltpu.VMEM((2,) + dense, I32),
            pltpu.VMEM(dense, I32),
            pltpu.VMEM(dense, I32),
            pltpu.SMEM(dense, I32),
            pltpu.SMEM(dense, I32),
            pltpu.VMEM((544, LANES), F32),
            pltpu.VMEM((96, LANES), F32),
            pltpu.VMEM((384, 256), BF16),
            pltpu.VMEM((288, LANES), F32),
            pltpu.VMEM((1056, LANES), F32),
            pltpu.VMEM((4096, 256), F32),
            pltpu.VMEM((4096, 384), F32),
            pltpu.VMEM((4096, 256), F32),
            pltpu.VMEM((BACK * LANES, 1024), BF16),
            pltpu.VMEM((BACK * LANES, 1024), BF16),
            pltpu.VMEM((LANES, 1024), BF16),
            pltpu.VMEM((288, LANES), F32),
            pltpu.VMEM((288, LANES), F32),
            pltpu.VMEM((576, 512), BF16),
            pltpu.VMEM((576, 512), BF16),
            pltpu.VMEM((288, LANES), F32),
            pltpu.SemaphoreType.DMA((4,)),
            pltpu.SemaphoreType.DMA((4,)),
            pltpu.SemaphoreType.DMA((2 * CHUNKS,)),
            pltpu.SemaphoreType.DMA((2,)),
        ],
        compiler_params=pltpu.CompilerParams(
            vmem_limit_bytes=VMEM_LIMIT, collective_id=0, has_side_effects=True
        ),
        name="main",
    )(params, lists_next, lists_cur, jnp.transpose(angles_next), jnp.transpose(angles_cur), counts_next, counts_cur,
      jnp.transpose(sends_next[0]), jnp.transpose(sends_cur[0]), jnp.transpose(cotangent, (1, 0, 2)), power, moments)
    grads, image = pl.pallas_call(
        scatter_kernel,
        out_shape=(shape((ROWS, GAUSS)), shape((3, 16, 256))),
        in_specs=[VM] * 3 + [pl.BlockSpec(memory_space=pl.ANY)],
        out_specs=(pl.BlockSpec(memory_space=pl.ANY),) * 2,
        scratch_shapes=[
            pltpu.VMEM(dense, I32),
            pltpu.VMEM(dense, I32),
            pltpu.SMEM(dense, I32),
            pltpu.VMEM((HALF, LANES), F32),
            pltpu.VMEM((2, 64, LANES), F32),
            pltpu.VMEM((2, LANES, LANES), F32),
            pltpu.VMEM((ROWS, GAUSS), F32),
            pltpu.SemaphoreType.DMA,
            pltpu.SemaphoreType.DMA,
            pltpu.SemaphoreType.DMA((2 * CHUNKS,)),
        ],
        compiler_params=PARAMS,
        name="scatter",
    )(returned, basis, jnp.transpose(sends_cur[0]), image)
    return jnp.transpose(image, (1, 0, 2)), grads


def solution(mesh):
    both = ("gauss", "pix")
    placed = (
        P(None, both),
        P(both, None),
        P(both, None),
        P(both, None),
        P(both, None),
        P(both),
        P(both),
        P(both, None, None),
        P(both, None, None),
        P(both, None, None),
    )
    return jax.shard_map(
        body,
        mesh=mesh,
        in_specs=placed,
        out_specs=(P(both, None, None), P(None, both)),
        check_vma=False,
    )
```
